32 devices in a mesh: row: 4 (over y, core), col: 8 (over z, x).
Axes of the slice: x: 2, y: 2, z: 4, core: 2. Of those that a mesh axis runs over, the one named last changes fastest.
Arguments:
- tokens: bfloat16 [64, 8192], P('col', 'row'), may hold values from -6 to 6
- up_blocks: bfloat16 [4, 8, 112, 128, 128], P('row', 'col'), may hold values from -0.1875 to 0.1875
- up_index: int32 [4, 8, 112], P('row', 'col'), may hold values from 0 to 448, as said below
- down_blocks: bfloat16 [4, 8, 112, 128, 128], P('row', 'col'), may hold values from -0.09375 to 0.09375
- down_index: int32 [4, 8, 112], P('row', 'col'), may hold values from 0 to 448, as said below
- out_cot: bfloat16 [64, 8192], P('col', 'row'), may hold values from -1.5 to 1.5
Outputs:
- outputs: bfloat16 [64, 8192], P('col', 'row')
- input_grad: bfloat16 [64, 8192], P('col', 'row')
- up_grad: bfloat16 [4, 8, 112, 128, 128], P('row', 'col')
- down_grad: bfloat16 [4, 8, 112, 128, 128], P('row', 'col')
The draws below stay inside these ranges and needn't reach their ends.
Inputs may be any that keep to these rules, and one draw needn't show every extreme that they name: `up_index`: each entry names a block of its tile's 16 x 28 grid as row * 28 + column, or is 448 for an empty slot; the named blocks of a tile are distinct and come before its empty slots; every tile names at least one block; the tiles (r, c) with c * 4 // 8 == r name 112 blocks, every other tile fewer. `down_index`: each entry names a block of its tile's 28 x 16 grid (hidden-unit block, width block) as row * 16 + column, or is 448 for an empty slot; the named blocks of a tile are distinct and come before its empty slots; every tile names at least one block; the tiles (r, c) with c * 4 // 8 == r name 112 blocks, every other tile fewer.
All inputs are finite; a program needn't handle non-finite values.
Results may differ from the reference program's by a relative error of at most 0.023.
Values may be sent and summed in bfloat16 or wider, within the bound.
No kernel may reach another device: no remote copies, remote signals or barrier semaphores. Data moves between devices by JAX's collectives and lax.ppermute only.
A program may use at most 64 MiB of HBM per device.

```python
import jax
import jax.numpy as jnp
from jax import lax

D = 8192
FF = 28672
BS = 128
GRID_R = 4
GRID_C = 8
TOKENS = 64
RB = 16
CB = 28
MOST = 112


def tile_pattern(key):
    count_all = RB * CB
    row_ids = jnp.arange(GRID_R, dtype=jnp.int32)[:, None]
    col_ids = jnp.arange(GRID_C, dtype=jnp.int32)[None, :]
    diagonal = col_ids * GRID_R // GRID_C == row_ids
    count_key, order_key = jax.random.split(key)
    counts = jax.random.randint(count_key, (GRID_R, GRID_C), 1, MOST, dtype=jnp.int32)
    counts = jnp.where(diagonal, MOST, counts)
    subkeys = jax.random.split(order_key, GRID_R * GRID_C)
    orders = jax.vmap(lambda subkey: jax.random.permutation(subkey, count_all))(subkeys)
    orders = orders.reshape(GRID_R, GRID_C, count_all)[:, :, :MOST].astype(jnp.int32)
    slots = jnp.arange(MOST, dtype=jnp.int32)
    return jnp.where(slots[None, None, :] < counts[:, :, None], orders, count_all).astype(jnp.int32)


def draw_up_index(key, part):
    return tile_pattern(jax.random.fold_in(key, 11))


def draw_down_index(key, part):
    return tile_pattern(jax.random.fold_in(key, 23))


def steps_of(rng, shape, cuts, low, top_value):
    def one(axis_at, blocks):
        draws = jax.random.uniform(jax.random.fold_in(jax.random.fold_in(rng, 6), axis_at), (blocks,), jnp.float32, low / len(cuts), top_value / len(cuts))
        return jnp.repeat(jnp.exp(draws), shape[axis_at] // blocks).reshape((-1,) + (1,) * (len(shape) - axis_at - 1))

    gain = one(*cuts[0])
    for cut in cuts[1:]:
        gain = gain * one(*cut)
    return gain


def normal_values(stream_key, extent, scale, most, cuts=(), kind=jnp.bfloat16):
    loudness = steps_of(stream_key, extent, cuts, -0.22, 0.18) if cuts else 1.0
    array = jax.random.normal(stream_key, extent, jnp.float32) * scale * loudness
    return jnp.minimum(jnp.maximum(array, -most), most).astype(kind)


def setup_inputs(seed: int = 0) -> dict:
    key_of = jax.random.split(jax.random.key(seed), 7)
    return {
        "tokens": normal_values(key_of[0], (TOKENS, D), 1.0, 6.0, ((0, 8), (1, 4))),
        "up_blocks": normal_values(key_of[1], (GRID_R, GRID_C, MOST, BS, BS), (D // 8) ** -0.5, 0.1875, ((0, 4), (1, 8))),
        "up_index": draw_up_index(jax.random.fold_in(key_of[6], 71), 0),
        "down_blocks": normal_values(key_of[3], (GRID_R, GRID_C, MOST, BS, BS), (FF // 8) ** -0.5, 0.09375, ((0, 4), (1, 8))),
        "down_index": draw_down_index(jax.random.fold_in(key_of[6], 71), 0),
        "out_cot": normal_values(key_of[5], (TOKENS, D), 0.25, 1.5, ((0, 8), (1, 4))),
    }


COEF = 0.7978845608
CUBIC = 0.044715


def gelu_value(values):
    inner = COEF * (values + CUBIC * values * values * values)
    return 0.5 * values * (1.0 + jnp.tanh(inner))


def gelu_slope(values):
    tangent = jnp.tanh(COEF * (values + CUBIC * values * values * values))
    return 0.5 * (1.0 + tangent) + 0.5 * values * (1.0 - tangent * tangent) * COEF * (1.0 + 3.0 * CUBIC * values * values)


def selectors(indices, leading, trailing):
    lead_pos = indices // trailing
    trail_pos = indices % trailing
    lead_sel = (lead_pos[:, None] == jnp.arange(leading, dtype=jnp.int32)[None, :]).astype(jnp.float32)
    trail_sel = (trail_pos[:, None] == jnp.arange(trailing, dtype=jnp.int32)[None, :]).astype(jnp.float32)
    return lead_sel, trail_sel


def forward_tile(operand, blocks, indices, leading, trailing):
    lead_sel, trail_sel = selectors(indices, leading, trailing)
    tok_count = operand.shape[0]
    pieces = operand.astype(jnp.float32).reshape(tok_count, leading, BS)
    picked = jnp.einsum('tab,ka->ktb', pieces, lead_sel, precision=lax.Precision.HIGHEST)
    products = jnp.einsum('ktb,kbd->ktd', picked, blocks.astype(jnp.float32), precision=lax.Precision.HIGHEST)
    result = jnp.einsum('ktd,kc->tcd', products, trail_sel, precision=lax.Precision.HIGHEST)
    return result.reshape(tok_count, trailing * BS)


def backward_tile(other, blocks, indices, leading, trailing):
    lead_sel, trail_sel = selectors(indices, leading, trailing)
    tok_count = other.shape[0]
    pieces = other.astype(jnp.float32).reshape(tok_count, trailing, BS)
    picked = jnp.einsum('tcd,kc->ktd', pieces, trail_sel, precision=lax.Precision.HIGHEST)
    products = jnp.einsum('ktd,kbd->ktb', picked, blocks.astype(jnp.float32), precision=lax.Precision.HIGHEST)
    result = jnp.einsum('ktb,ka->tab', products, lead_sel, precision=lax.Precision.HIGHEST)
    return result.reshape(tok_count, leading * BS)


def grad_tile(operand, other, indices, leading, trailing):
    lead_sel, trail_sel = selectors(indices, leading, trailing)
    tok_count = operand.shape[0]
    left_pick = jnp.einsum('tab,ka->ktb', operand.astype(jnp.float32).reshape(tok_count, leading, BS), lead_sel, precision=lax.Precision.HIGHEST)
    right_pick = jnp.einsum('tcd,kc->ktd', other.astype(jnp.float32).reshape(tok_count, trailing, BS), trail_sel, precision=lax.Precision.HIGHEST)
    return jnp.einsum('ktb,ktd->kbd', left_pick, right_pick, precision=lax.Precision.HIGHEST)


def rounded(values):
    return lax.optimization_barrier(values.astype(jnp.bfloat16)).astype(jnp.float32)


def reference(tokens, up_blocks, up_index, down_blocks, down_index, out_cot):
    tok_count = tokens.shape[0]
    by_row = tokens.reshape(tok_count, GRID_R, RB * BS).transpose(1, 0, 2)
    cot_by_row = out_cot.reshape(tok_count, GRID_R, RB * BS).transpose(1, 0, 2)
    up_by_col = jnp.swapaxes(up_blocks, 0, 1)
    up_index_col = jnp.swapaxes(up_index, 0, 1)
    down_by_col = jnp.swapaxes(down_blocks, 0, 1)
    down_index_col = jnp.swapaxes(down_index, 0, 1)

    def up_step(running, inputs):
        feats, blocks_row, index_row = inputs
        terms = jax.vmap(lambda blk, ind: forward_tile(feats, blk, ind, RB, CB))(blocks_row, index_row)
        return running + rounded(terms), None

    preact, _ = lax.scan(up_step, jnp.zeros((GRID_C, tok_count, CB * BS), jnp.float32), (by_row, up_blocks, up_index))
    hidden = gelu_value(preact).astype(jnp.bfloat16)

    def down_step(running, inputs):
        hidden_col, blocks_col, index_col = inputs
        terms = jax.vmap(lambda blk, ind: forward_tile(hidden_col, blk, ind, CB, RB))(blocks_col, index_col)
        return running + rounded(terms), None

    out_sum, _ = lax.scan(down_step, jnp.zeros((GRID_R, tok_count, RB * BS), jnp.float32), (hidden, down_by_col, down_index_col))
    outputs = out_sum.transpose(1, 0, 2).reshape(tok_count, D).astype(jnp.bfloat16)

    def act_step(running, inputs):
        cot_row, blocks_row, index_row = inputs
        terms = jax.vmap(lambda blk, ind: backward_tile(cot_row, blk, ind, CB, RB))(blocks_row, index_row)
        return running + rounded(terms), None

    act_grad, _ = lax.scan(act_step, jnp.zeros((GRID_C, tok_count, CB * BS), jnp.float32), (cot_by_row, down_blocks, down_index))
    pre_grad = (act_grad * gelu_slope(preact)).astype(jnp.bfloat16)

    def input_step(running, inputs):
        grad_col, blocks_col, index_col = inputs
        terms = jax.vmap(lambda blk, ind: backward_tile(grad_col, blk, ind, RB, CB))(blocks_col, index_col)
        return running + rounded(terms), None

    in_sum, _ = lax.scan(input_step, jnp.zeros((GRID_R, tok_count, RB * BS), jnp.float32), (pre_grad, up_by_col, up_index_col))
    input_grad = in_sum.transpose(1, 0, 2).reshape(tok_count, D).astype(jnp.bfloat16)

    def up_grad_row(inputs):
        feats, index_row = inputs
        return jax.vmap(lambda grad_col, ind: grad_tile(feats, grad_col, ind, RB, CB))(pre_grad, index_row)

    up_grad = lax.map(up_grad_row, (by_row, up_index)).astype(jnp.bfloat16)

    def down_grad_row(inputs):
        cot_row, index_row = inputs
        return jax.vmap(lambda hidden_col, ind: grad_tile(hidden_col, cot_row, ind, CB, RB))(hidden, index_row)

    down_grad = lax.map(down_grad_row, (cot_by_row, down_index)).astype(jnp.bfloat16)
    return (outputs, input_grad, up_grad, down_grad)
```

```python
import functools

import jax
import jax.numpy as jnp
from jax import lax
from jax.experimental import pallas as pl
from jax.experimental.pallas import tpu as pltpu
from jax.sharding import PartitionSpec as P

FF = 28672
BS = 128
COEF = 0.7978845608
CUBIC = 0.044715
F32 = jnp.float32
BF16 = jnp.bfloat16
VMEM = pl.BlockSpec(memory_space=pltpu.VMEM)
SMEM = pl.BlockSpec(memory_space=pltpu.SMEM)


def gelu_value(values):
    inner = COEF * (values + CUBIC * values * values * values)
    return 0.5 * values * (1.0 + jnp.tanh(inner))


def gelu_slope(values):
    tangent = jnp.tanh(COEF * (values + CUBIC * values * values * values))
    return 0.5 * (1.0 + tangent) + 0.5 * values * (1.0 - tangent * tangent) * COEF * (
        1.0 + 3.0 * CUBIC * values * values
    )


def params(megabytes=24):
    return pltpu.CompilerParams(vmem_limit_bytes=megabytes << 20)


def divisor(count, most):
    return max(step for step in range(1, most + 1) if count % step == 0)


def accumulate(index_ref, leading, trailing, forward, operand_ref, blocks_ref, acc):
    acc[...] = jnp.zeros_like(acc)
    slots = index_ref.shape[0]
    step = divisor(slots, 28)
    targets = trailing if forward else leading

    def group(at, carry):
        products = []
        for inner in range(step):
            slot = at * step + inner
            place = index_ref[slot]
            named = place < leading * trailing
            lead, trail = jnp.minimum(place // trailing, leading - 1), place % trailing
            source, target = (lead, trail) if forward else (trail, lead)
            dims = (((1,), (0 if forward else 1,)), ((), ()))
            product = lax.dot_general(
                operand_ref[source], blocks_ref[slot], dims, preferred_element_type=F32
            )
            products.append((jnp.where(named, target, targets), product))
        for target, product in products:
            acc[target] += product
        return carry

    lax.fori_loop(0, slots // step, group, 0)


def split_halves(core, acc, targets, keep_ref, give_ref):
    half = acc.shape[1] // 2
    for at in range(targets):
        keep_ref[at] = acc[at, pl.ds(pl.multiple_of(core * half, half), half), :].astype(BF16)
        give_ref[at] = acc[at, pl.ds(pl.multiple_of((1 - core) * half, half), half), :].astype(BF16)


def up_kernel(leading, trailing, *refs):
    core_ref, index_ref, blocks_ref = refs[:3]
    parts = refs[3:-5]
    tokens_ref, cot_ref, keep_ref, give_ref, acc = refs[-5:]
    rows = parts[0].shape[0] // 2
    for pair in range(len(parts) // 2):
        here = pl.ds(pair * 2 * rows, 2 * rows)
        for at in range(leading):
            lanes = pl.ds(at * BS, BS)
            first = parts[2 * pair][:, lanes].astype(F32)
            second = parts[2 * pair + 1][:, lanes].astype(F32)
            tokens_ref[at, here, :] = jnp.concatenate([first[:rows], second[:rows]]).astype(BF16)
            cot_ref[at, here, :] = jnp.concatenate([first[rows:], second[rows:]]).astype(BF16)
    accumulate(index_ref, leading, trailing, True, tokens_ref, blocks_ref, acc)
    split_halves(core_ref[0], acc, trailing, keep_ref, give_ref)


def act_kernel(leading, trailing, core_ref, index_ref, blocks_ref, cot_ref, keep_ref, give_ref, acc):
    accumulate(index_ref, leading, trailing, False, cot_ref, blocks_ref, acc)
    split_halves(core_ref[0], acc, leading, keep_ref, give_ref)


def join_halves(core, own_ref, other_ref, whole_ref):
    half = own_ref.shape[1]
    for at in range(own_ref.shape[0]):
        whole_ref[at, pl.ds(pl.multiple_of(core * half, half), half), :] = own_ref[at]
        whole_ref[at, pl.ds(pl.multiple_of((1 - core) * half, half), half), :] = other_ref[at]


def down_kernel(
    leading, trailing, core_ref, index_ref, blocks_ref, own_ref, other_ref, hidden_ref, terms_ref, acc
):
    join_halves(core_ref[0], own_ref, other_ref, hidden_ref)
    accumulate(index_ref, leading, trailing, True, hidden_ref, blocks_ref, acc)
    for at in range(trailing):
        terms_ref[at] = acc[at].astype(BF16)


def input_kernel(
    leading, trailing, core_ref, index_ref, blocks_ref, own_ref, other_ref, out_terms_ref, grad_ref, *refs
):
    chunks, acc = refs[:-1], refs[-1]
    join_halves(core_ref[0], own_ref, other_ref, grad_ref)
    accumulate(index_ref, leading, trailing, False, grad_ref, blocks_ref, acc)
    rows = chunks[0].shape[0] // 2
    for at in range(leading):
        for pair in range(len(chunks) // 2):
            here = pl.ds(pair * 2 * rows, 2 * rows)
            outs = out_terms_ref[at, here, :].astype(F32)
            grads = acc[at, here, :]
            for inner in range(2):
                mine = slice(inner * rows, (inner + 1) * rows)
                chunks[2 * pair + inner][:, pl.ds(at * BS, BS)] = jnp.concatenate(
                    [outs[mine], grads[mine]]
                ).astype(BF16)


def grad_kernel(leading, trailing, step, index_ref, left_ref, right_ref, out_ref, turned):
    @pl.when(pl.program_id(0) == 0)
    def _():
        for at in range(leading):
            turned[at] = left_ref[at].T

    for inner in range(step):
        place = index_ref[pl.program_id(0) * step + inner]
        lead, trail = jnp.minimum(place // trailing, leading - 1), place % trailing
        product = jnp.dot(turned[lead], right_ref[trail], preferred_element_type=F32)
        out_ref[inner] = jnp.where(place < leading * trailing, product, 0.0).astype(BF16)


def block_grads(name, index, left, right):
    leading, tok_count, _ = left.shape
    trailing = right.shape[0]
    slots = index.shape[0]
    step = divisor(slots, 16)
    return pl.pallas_call(
        functools.partial(grad_kernel, leading, trailing, step),
        grid=(slots // step,),
        out_shape=jax.ShapeDtypeStruct((slots, BS, BS), BF16),
        in_specs=[SMEM, VMEM, VMEM],
        out_specs=pl.BlockSpec((step, BS, BS), lambda at: (at, 0, 0)),
        scratch_shapes=[pltpu.VMEM((leading, BS, tok_count), BF16)],
        compiler_params=params(),
        cost_estimate=pl.CostEstimate(
            flops=2 * slots * BS * BS * tok_count, bytes_accessed=2 * slots * BS * BS, transcendentals=0
        ),
        name=name,
    )(index, left, right)


def shards(tokens, up_blocks, up_index, down_blocks, down_index, out_cot):
    rows, width = tokens.shape
    col_devices, row_devices = lax.axis_size("col"), lax.axis_size("row")
    row_blocks = width // BS
    col_blocks = FF // (BS * col_devices)
    tok_count = rows * col_devices
    half = tok_count // 2
    slots = up_index.shape[2]
    up_weight, down_weight = up_blocks[0, 0], down_blocks[0, 0]
    up_place, down_place = up_index[0, 0], down_index[0, 0]
    core = (lax.axis_index("row") % 2).astype(jnp.int32).reshape(1)

    def swap(values, axis, bit):
        count = lax.axis_size(axis)
        return lax.ppermute(values, axis, [(at, at ^ bit) for at in range(count)])

    def cost(blocks):
        return pl.CostEstimate(
            flops=2 * slots * BS * BS * tok_count, bytes_accessed=2 * slots * BS * BS, transcendentals=0
        )

    mine = jnp.concatenate([tokens, out_cot], axis=0)
    parts = [mine] + [swap(mine, "col", bit) for bit in range(1, col_devices)]

    tile_rows = jax.ShapeDtypeStruct((row_blocks, tok_count, BS), BF16)
    tile_cols = jax.ShapeDtypeStruct((col_blocks, tok_count, BS), BF16)
    half_cols = jax.ShapeDtypeStruct((col_blocks, half, BS), BF16)
    acc_rows = pltpu.VMEM((row_blocks + 1, tok_count, BS), F32)
    acc_cols = pltpu.VMEM((col_blocks + 1, tok_count, BS), F32)

    def summed(keep, give):
        total = (keep.astype(F32) + swap(give, "row", 1).astype(F32)).astype(BF16)
        bit = 2
        while bit < row_devices:
            other = swap(total, "row", bit)
            whole = total.astype(F32) + other.astype(F32)
            total = whole.astype(BF16)
            bit *= 2
        return whole

    features, cotangents, pre_keep, pre_give = pl.pallas_call(
        functools.partial(up_kernel, row_blocks, col_blocks),
        out_shape=(tile_rows, tile_rows, half_cols, half_cols),
        in_specs=[SMEM, SMEM] + [VMEM] * (1 + len(parts)),
        out_specs=(VMEM,) * 4,
        scratch_shapes=[acc_cols],
        compiler_params=params(),
        cost_estimate=cost(up_weight),
        name="up",
    )(core, up_place, up_weight, *parts)
    preact = summed(pre_keep, pre_give)

    act_keep, act_give = pl.pallas_call(
        functools.partial(act_kernel, col_blocks, row_blocks),
        out_shape=(half_cols, half_cols),
        in_specs=[SMEM, SMEM, VMEM, VMEM],
        out_specs=(VMEM,) * 2,
        scratch_shapes=[acc_cols],
        compiler_params=params(),
        cost_estimate=cost(down_weight),
        name="act",
    )(core, down_place, down_weight, cotangents)
    act_grad = summed(act_keep, act_give)

    hidden_own = gelu_value(preact).astype(BF16)
    slope = gelu_slope(preact)
    hidden, out_terms = pl.pallas_call(
        functools.partial(down_kernel, col_blocks, row_blocks),
        out_shape=(tile_cols, tile_rows),
        in_specs=[SMEM, SMEM, VMEM, VMEM, VMEM],
        out_specs=(VMEM,) * 2,
        scratch_shapes=[acc_rows],
        compiler_params=params(),
        cost_estimate=cost(down_weight),
        name="down",
    )(core, down_place, down_weight, hidden_own, swap(hidden_own, "row", 1))

    grad_own = (act_grad * slope).astype(BF16)
    chunk = jax.ShapeDtypeStruct((2 * rows, width), BF16)
    pre_grad, *chunks = pl.pallas_call(
        functools.partial(input_kernel, row_blocks, col_blocks),
        out_shape=(tile_cols,) + (chunk,) * col_devices,
        in_specs=[SMEM, SMEM, VMEM, VMEM, VMEM, VMEM],
        out_specs=(VMEM,) * (1 + col_devices),
        scratch_shapes=[acc_rows],
        compiler_params=params(),
        cost_estimate=cost(up_weight),
        name="input",
    )(core, up_place, up_weight, grad_own, swap(grad_own, "row", 1), out_terms)
    total = chunks[0].astype(F32)
    for bit in range(1, col_devices):
        total = total + swap(chunks[bit], "col", bit).astype(F32)
    total = total.astype(BF16)

    up_grad = block_grads("up_grad", up_place, features, pre_grad)
    down_grad = block_grads("down_grad", down_place, hidden, cotangents)
    return total[:rows], total[rows:], up_grad[None, None], down_grad[None, None]


def solution(mesh):
    placed = (
        P("col", "row"),
        P("row", "col", None, None, None),
        P("row", "col", None),
        P("row", "col", None, None, None),
        P("row", "col", None),
        P("col", "row"),
    )
    return jax.shard_map(
        shards,
        mesh=mesh,
        in_specs=placed,
        out_specs=(
            P("col", "row"),
            P("col", "row"),
            P("row", "col", None, None, None),
            P("row", "col", None, None, None),
        ),
        check_vma=False,
    )
```

```python
import functools

import jax
import jax.numpy as jnp
from jax import lax
from jax.experimental import pallas as pl
from jax.experimental.pallas import tpu as pltpu
from jax.sharding import PartitionSpec as P

FF = 28672
BS = 128
COEF = 0.7978845608
CUBIC = 0.044715
F32 = jnp.float32
BF16 = jnp.bfloat16
VMEM = pl.BlockSpec(memory_space=pltpu.VMEM)
SMEM = pl.BlockSpec(memory_space=pltpu.SMEM)
HBM = pl.BlockSpec(memory_space=pltpu.HBM)


def gelu_value(values):
    inner = COEF * (values + CUBIC * values * values * values)
    return 0.5 * values * (1.0 + jnp.tanh(inner))


def gelu_slope(values):
    tangent = jnp.tanh(COEF * (values + CUBIC * values * values * values))
    return 0.5 * (1.0 + tangent) + 0.5 * values * (1.0 - tangent * tangent) * COEF * (
        1.0 + 3.0 * CUBIC * values * values
    )


def params(megabytes=24):
    return pltpu.CompilerParams(vmem_limit_bytes=megabytes << 20)


def divisor(count, most):
    return max(step for step in range(1, most + 1) if count % step == 0)


class Stream:
    def __init__(self, index_hbm, blocks_hbm, index_ref, blocks_ref, index_sem, sems):
        self.index, self.blocks = index_ref, blocks_ref
        self.index_copy = pltpu.make_async_copy(index_hbm, index_ref, index_sem)
        self.step = blocks_ref.shape[0] // sems.shape[0]
        self.copies = lambda at: pltpu.make_async_copy(
            blocks_hbm.at[pl.ds(at * self.step, self.step)],
            blocks_ref.at[pl.ds(at * self.step, self.step)],
            sems.at[at],
        )
        self.index_copy.start()
        for at in range(sems.shape[0]):
            self.copies(at).start()

    @staticmethod
    def scratch(slots, most):
        return [
            pltpu.SMEM((slots,), jnp.int32),
            pltpu.VMEM((slots, BS, BS), BF16),
            pltpu.SemaphoreType.DMA,
            pltpu.SemaphoreType.DMA((slots // divisor(slots, most),)),
        ]

    def prepare(self):
        self.index_copy.wait()

    def group(self, at):
        self.copies(at).wait()


class Held:
    def __init__(self, index_ref, blocks_ref, most):
        self.index, self.blocks = index_ref, blocks_ref
        self.step = divisor(blocks_ref.shape[0], most)

    def prepare(self):
        pass

    def group(self, at):
        pass


def accumulate(source, leading, trailing, operand_ref, acc):
    acc[...] = jnp.zeros_like(acc)
    source.prepare()

    def group(at, carry):
        source.group(at)
        products = []
        for inner in range(source.step):
            slot = at * source.step + inner
            place = source.index[slot]
            lead = jnp.minimum(place // trailing, leading - 1)
            trail = jnp.where(place < leading * trailing, place % trailing, trailing)
            products.append(
                (trail, jnp.dot(operand_ref[lead], source.blocks[slot], preferred_element_type=F32))
            )
        for trail, product in products:
            acc[trail] += product
        return carry

    lax.fori_loop(0, source.blocks.shape[0] // source.step, group, 0)


def accumulate_turned(source, leading, trailing, operand_ref, turned, acc):
    for at in range(trailing):
        turned[at] = operand_ref[at].T
    acc[...] = jnp.zeros_like(acc)
    source.prepare()

    def group(at, carry):
        source.group(at)
        products = []
        for inner in range(source.step):
            slot = at * source.step + inner
            place = source.index[slot]
            named = place < leading * trailing
            lead = jnp.where(named, place // trailing, leading)
            products.append(
                (lead, jnp.dot(source.blocks[slot], turned[place % trailing], preferred_element_type=F32))
            )
        for lead, product in products:
            acc[lead] += product
        return carry

    lax.fori_loop(0, source.blocks.shape[0] // source.step, group, 0)


def split_halves(core, read, targets, keep_ref, give_ref):
    half = keep_ref.shape[1]
    for at in range(targets):
        low, high = read(at, 0), read(at, half)
        keep_ref[at] = jnp.where(core == 0, low, high).astype(BF16)
        give_ref[at] = jnp.where(core == 0, high, low).astype(BF16)


def position(axis):
    return lax.axis_index(axis).astype(jnp.int32)


def core():
    return position("row") % 2


def pack_kernel(tokens_ref, cot_ref, mine_ref, held, sems):
    copies = [
        pltpu.make_async_copy(source, held.at[at], sems.at[at])
        for at, source in enumerate((tokens_ref, cot_ref))
    ]
    for copy in copies:
        copy.start()
    for copy in copies:
        copy.wait()
    mine_ref[...] = jnp.concatenate([held[0].astype(F32), held[1].astype(F32)]).astype(BF16)


def up_kernel(leading, trailing, index_hbm, blocks_hbm, *refs):
    parts = refs[:-9]
    tokens_ref, cot_ref, keep_ref, give_ref, acc = refs[-9:-4]
    source = Stream(index_hbm, blocks_hbm, *refs[-4:])
    rows = parts[0].shape[0] // 2
    for pair in range(len(parts) // 2):
        here = pl.ds(pair * 2 * rows, 2 * rows)
        for at in range(leading):
            lanes = pl.ds(at * BS, BS)
            first = parts[2 * pair][:, lanes].astype(F32)
            second = parts[2 * pair + 1][:, lanes].astype(F32)
            tokens_ref[at, here, :] = jnp.concatenate([first[:rows], second[:rows]]).astype(BF16)
            cot_ref[at, here, :] = jnp.concatenate([first[rows:], second[rows:]]).astype(BF16)
    accumulate(source, leading, trailing, tokens_ref, acc)
    half = keep_ref.shape[1]
    split_halves(core(), lambda at, low: acc[at, low : low + half, :], trailing, keep_ref, give_ref)


def act_kernel(
    leading, trailing, index_ref, blocks_ref, cot_ref, after_ref, keep_ref, give_ref, turned, acc
):
    accumulate_turned(Held(index_ref, blocks_ref, 56), leading, trailing, cot_ref, turned, acc)
    half = keep_ref.shape[1]

    def read(at, low):
        return acc[at].T[low : low + half]

    split_halves(core(), read, leading, keep_ref, give_ref)


def join_halves(core, own_ref, other_ref, whole_ref):
    half = own_ref.shape[1]
    for at in range(own_ref.shape[0]):
        own, other = own_ref[at], other_ref[at]
        whole_ref[at, :half, :] = jnp.where(core == 0, own, other)
        whole_ref[at, half:, :] = jnp.where(core == 0, other, own)


def gelu_kernel(own_ref, other_ref, hidden_ref, slope_ref):
    for at in range(own_ref.shape[0]):
        preact = own_ref[at].astype(F32) + other_ref[at].astype(F32)
        hidden_ref[at] = gelu_value(preact).astype(BF16)
        slope_ref[at] = gelu_slope(preact)


def slope_kernel(own_ref, other_ref, slope_ref, grad_ref):
    for at in range(own_ref.shape[0]):
        act_grad = own_ref[at].astype(F32) + other_ref[at].astype(F32)
        grad_ref[at] = (act_grad * slope_ref[at]).astype(BF16)


def down_kernel(
    leading, trailing, index_ref, blocks_ref, own_ref, other_ref, hidden_ref, terms_ref, acc
):
    join_halves(core(), own_ref, other_ref, hidden_ref)
    accumulate(Held(index_ref, blocks_ref, 56), leading, trailing, hidden_ref, acc)
    devices, rows, _ = terms_ref.shape
    for device in range(devices):
        here = pl.multiple_of(jnp.bitwise_xor(position("col"), device) * rows, rows)
        for at in range(trailing):
            terms_ref[device, :, pl.ds(at * BS, BS)] = acc[at, pl.ds(here, rows), :].astype(BF16)


def input_kernel(
    leading, trailing, index_hbm, blocks_hbm, own_ref, other_ref, grad_ref, terms_ref, turned, acc, flat, *stream
):
    source = Stream(index_hbm, blocks_hbm, *stream)
    join_halves(core(), own_ref, other_ref, grad_ref)
    accumulate_turned(source, leading, trailing, grad_ref, turned, acc)
    for at in range(leading):
        flat[at] = acc[at].T
    devices, rows, _ = terms_ref.shape
    for device in range(devices):
        here = pl.multiple_of(jnp.bitwise_xor(position("col"), device) * rows, rows)
        for at in range(leading):
            terms_ref[device, :, pl.ds(at * BS, BS)] = flat[at, pl.ds(here, rows), :].astype(BF16)


def block_grads(leading, trailing, index_ref, left_ref, right_ref, out_ref, turned, held, sems):
    slots = index_ref.shape[0]
    step = divisor(slots, 56)

    def out_copy(at):
        here = pl.ds(at * step, step)
        return pltpu.make_async_copy(held.at[here], out_ref.at[here], sems.at[at])

    for at in range(leading):
        turned[at] = left_ref[at].T

    def group(at, carry):
        for inner in range(step):
            slot = at * step + inner
            place = index_ref[slot]
            lead = jnp.minimum(place // trailing, leading - 1)
            product = jnp.dot(turned[lead], right_ref[place % trailing], preferred_element_type=F32)
            held[slot] = jnp.where(place < leading * trailing, product, 0.0).astype(BF16)
        out_copy(at).start()
        return carry

    lax.fori_loop(0, slots // step, group, 0)
    return [out_copy(at) for at in range(slots // step)]


def tail_kernel(
    up_index,
    down_index,
    tokens_ref,
    pre_grad_ref,
    hidden_ref,
    cot_ref,
    received_ref,
    up_ref,
    down_ref,
    outputs_ref,
    up_turned,
    down_turned,
    up_held,
    down_held,
    up_sems,
    down_sems,
):
    rows, cols = tokens_ref.shape[0], hidden_ref.shape[0]
    copies = block_grads(
        cols, rows, down_index, hidden_ref, cot_ref, down_ref, down_turned, down_held, down_sems
    )
    copies += block_grads(
        rows, cols, up_index, tokens_ref, pre_grad_ref, up_ref, up_turned, up_held, up_sems
    )
    total = received_ref[0].astype(F32)
    for device in range(1, received_ref.shape[0]):
        total += received_ref[device].astype(F32)
    outputs_ref[...] = total.astype(BF16)
    for copy in copies:
        copy.wait()


def shards(tokens, up_blocks, up_index, down_blocks, down_index, out_cot):
    rows, width = tokens.shape
    col_devices, row_devices = lax.axis_size("col"), lax.axis_size("row")
    row_blocks = width // BS
    col_blocks = FF // (BS * col_devices)
    tok_count = rows * col_devices
    half = tok_count // 2
    slots = up_index.shape[2]
    up_weight = pltpu.with_memory_space_constraint(up_blocks[0, 0], pltpu.HBM)
    down_weight = down_blocks[0, 0]
    up_place = pltpu.with_memory_space_constraint(up_index[0, 0], pltpu.HBM)
    down_place = down_index[0, 0]
    cost = pl.CostEstimate(
        flops=2 * slots * BS * BS * tok_count, bytes_accessed=2 * slots * BS * BS, transcendentals=0
    )

    def swap(values, axis, bit):
        count = lax.axis_size(axis)
        return lax.ppermute(values, axis, [(at, at ^ bit) for at in range(count)])

    def call(body, name, outs, ins, scratch, *args, out_specs=None, **more):
        return pl.pallas_call(
            body,
            out_shape=outs,
            in_specs=ins,
            out_specs=out_specs or jax.tree.map(lambda _: VMEM, outs),
            scratch_shapes=scratch,
            compiler_params=params(),
            name=name,
            **more,
        )(*args)

    def shape(*dims, dtype=BF16):
        return jax.ShapeDtypeStruct(dims, dtype)

    long = pl.CostEstimate(flops=0, bytes_accessed=1 << 25, transcendentals=0)
    mine = call(
        pack_kernel,
        "pack",
        shape(2 * rows, width),
        [HBM] * 2,
        [pltpu.VMEM((2, rows, width), BF16), pltpu.SemaphoreType.DMA((2,))],
        pltpu.with_memory_space_constraint(tokens, pltpu.HBM),
        pltpu.with_memory_space_constraint(out_cot, pltpu.HBM),
        cost_estimate=long,
    )
    parts = {0: mine}
    for bit in sorted(range(1, col_devices), key=lambda bit: (bit < 4, bit % 2 if bit >= 4 else 0, bit)):
        relayed = bit >= 4 and bit % 2 == 1
        parts[bit] = swap(parts[bit - 1] if relayed else mine, "col", 1 if relayed else bit)
    parts = [parts[bit] for bit in range(col_devices)]

    tile_rows = shape(row_blocks, tok_count, BS)
    tile_cols = shape(col_blocks, tok_count, BS)
    half_cols = shape(col_blocks, half, BS)
    terms = shape(col_devices, rows, width)
    acc_rows = pltpu.VMEM((row_blocks + 1, tok_count, BS), F32)
    acc_cols = pltpu.VMEM((col_blocks + 1, tok_count, BS), F32)
    acc_rows_turned = pltpu.VMEM((row_blocks + 1, BS, tok_count), F32)
    acc_cols_turned = pltpu.VMEM((col_blocks + 1, BS, tok_count), F32)
    rows_turned = pltpu.VMEM((row_blocks, BS, tok_count), BF16)
    cols_turned = pltpu.VMEM((col_blocks, BS, tok_count), BF16)
    ANY = pl.BlockSpec(memory_space=pl.ANY)

    def pair_sum(keep, give, cut=1):
        parts = [swap(part, "row", 1) for part in jnp.split(give, cut)]
        total = (keep.astype(F32) + jnp.concatenate(parts).astype(F32)).astype(BF16)
        bit = 2
        while 2 * bit < row_devices:
            total = (total.astype(F32) + swap(total, "row", bit).astype(F32)).astype(BF16)
            bit *= 2
        return total

    last = row_devices // 2
    features, cotangents, pre_keep, pre_give = call(
        functools.partial(up_kernel, row_blocks, col_blocks),
        "up",
        (tile_rows, tile_rows, half_cols, half_cols),
        [HBM, HBM] + [VMEM] * len(parts),
        [acc_cols] + Stream.scratch(slots, 28),
        up_place,
        up_weight,
        *parts,
        cost_estimate=cost,
    )
    pre_own = pair_sum(pre_keep, pre_give)
    pre_other = swap(pre_own, "row", last)

    act_keep, act_give = call(
        functools.partial(act_kernel, col_blocks, row_blocks),
        "act",
        (half_cols, half_cols),
        [SMEM, VMEM, VMEM, ANY],
        [rows_turned, acc_cols_turned],
        down_place,
        down_weight,
        cotangents,
        pre_own,
        cost_estimate=cost,
    )
    act_own = pair_sum(act_keep, act_give)
    act_other = swap(act_own, "row", last)

    hidden_own, slope = call(
        gelu_kernel,
        "gelu",
        (half_cols, shape(col_blocks, half, BS, dtype=F32)),
        [VMEM, VMEM],
        [],
        pre_own,
        pre_other,
    )
    hidden, out_terms = call(
        functools.partial(down_kernel, col_blocks, row_blocks),
        "down",
        (tile_cols, terms),
        [SMEM, VMEM, VMEM, VMEM],
        [acc_rows],
        down_place,
        down_weight,
        hidden_own,
        swap(hidden_own, "row", 1),
        cost_estimate=cost,
    )

    def exchanged(values):
        return lax.all_to_all(values, "col", split_axis=0, concat_axis=0, tiled=True)

    out_received = exchanged(out_terms)
    grad_own = call(
        slope_kernel, "slope", half_cols, [VMEM] * 3, [], act_own, act_other, slope, cost_estimate=long
    )
    pre_grad, input_terms = call(
        functools.partial(input_kernel, row_blocks, col_blocks),
        "input",
        (tile_cols, terms),
        [HBM, HBM, VMEM, VMEM],
        [cols_turned, acc_rows_turned, pltpu.VMEM((row_blocks, tok_count, BS), F32)]
        + Stream.scratch(slots, 28),
        up_place,
        up_weight,
        grad_own,
        swap(grad_own, "row", 1),
        cost_estimate=cost,
    )
    input_grad = jnp.sum(exchanged(input_terms).astype(F32), axis=0).astype(BF16)
    chunks = pltpu.SemaphoreType.DMA((slots // divisor(slots, 56),))
    blocks = shape(slots, BS, BS)
    held = pltpu.VMEM((slots, BS, BS), BF16)
    up_grad, down_grad, outputs = call(
        tail_kernel,
        "tail",
        (blocks, blocks, shape(rows, width)),
        [SMEM, SMEM] + [VMEM] * 5,
        [rows_turned, cols_turned, held, held, chunks, chunks],
        up_index[0, 0],
        down_place,
        features,
        pre_grad,
        hidden,
        cotangents,
        out_received,
        out_specs=(HBM, HBM, VMEM),
        cost_estimate=pl.CostEstimate(
            flops=4 * slots * BS * BS * tok_count, bytes_accessed=4 * slots * BS * BS, transcendentals=0
        ),
    )
    return outputs, input_grad, up_grad[None, None], down_grad[None, None]


def solution(mesh):
    placed = (
        P("col", "row"),
        P("row", "col", None, None, None),
        P("row", "col", None),
        P("row", "col", None, None, None),
        P("row", "col", None),
        P("col", "row"),
    )
    return jax.shard_map(
        shards,
        mesh=mesh,
        in_specs=placed,
        out_specs=(
            P("col", "row"),
            P("col", "row"),
            P("row", "col", None, None, None),
            P("row", "col", None, None, None),
        ),
        check_vma=False,
    )
```

```python
import functools

import jax
import jax.numpy as jnp
from jax import lax
from jax.experimental import pallas as pl
from jax.experimental.pallas import tpu as pltpu
from jax.sharding import PartitionSpec as P

FF = 28672
BS = 128
COEF = 0.7978845608
CUBIC = 0.044715
F32 = jnp.float32
BF16 = jnp.bfloat16
VMEM = pl.BlockSpec(memory_space=pltpu.VMEM)
SMEM = pl.BlockSpec(memory_space=pltpu.SMEM)
HBM = pl.BlockSpec(memory_space=pltpu.HBM)


def gelu_value(values):
    inner = COEF * (values + CUBIC * values * values * values)
    return 0.5 * values * (1.0 + jnp.tanh(inner))


def gelu_slope(values):
    tangent = jnp.tanh(COEF * (values + CUBIC * values * values * values))
    return 0.5 * (1.0 + tangent) + 0.5 * values * (1.0 - tangent * tangent) * COEF * (
        1.0 + 3.0 * CUBIC * values * values
    )


def params(megabytes=24):
    return pltpu.CompilerParams(vmem_limit_bytes=megabytes << 20)


def divisor(count, most):
    return max(step for step in range(1, most + 1) if count % step == 0)


class Stream:
    def __init__(self, index_hbm, blocks_hbm, index_ref, blocks_ref, index_sem, sems):
        self.index, self.blocks = index_ref, blocks_ref
        self.index_copy = pltpu.make_async_copy(index_hbm, index_ref, index_sem)
        self.step = blocks_ref.shape[0] // sems.shape[0]
        self.copies = lambda at: pltpu.make_async_copy(
            blocks_hbm.at[pl.ds(at * self.step, self.step)],
            blocks_ref.at[pl.ds(at * self.step, self.step)],
            sems.at[at],
        )
        self.index_copy.start()
        for at in range(sems.shape[0]):
            self.copies(at).start()

    @staticmethod
    def scratch(slots, most):
        return [
            pltpu.SMEM((slots,), jnp.int32),
            pltpu.VMEM((slots, BS, BS), BF16),
            pltpu.SemaphoreType.DMA,
            pltpu.SemaphoreType.DMA((slots // divisor(slots, most),)),
        ]

    def prepare(self):
        self.index_copy.wait()

    def group(self, at):
        self.copies(at).wait()


class Held:
    def __init__(self, index_ref, blocks_ref, most):
        self.index, self.blocks = index_ref, blocks_ref
        self.step = divisor(blocks_ref.shape[0], most)

    def prepare(self):
        pass

    def group(self, at):
        pass


def accumulate(source, leading, trailing, operand_ref, acc):
    acc[...] = jnp.zeros_like(acc)
    source.prepare()

    def group(at, carry):
        source.group(at)
        products = []
        for inner in range(source.step):
            slot = at * source.step + inner
            place = source.index[slot]
            lead = jnp.minimum(place // trailing, leading - 1)
            trail = jnp.where(place < leading * trailing, place % trailing, trailing)
            products.append(
                (trail, jnp.dot(operand_ref[lead], source.blocks[slot], preferred_element_type=F32))
            )
        for trail, product in products:
            acc[trail] += product
        return carry

    lax.fori_loop(0, source.blocks.shape[0] // source.step, group, 0)


def accumulate_turned(source, leading, trailing, operand_ref, turned, acc):
    for at in range(trailing):
        turned[at] = operand_ref[at].T
    acc[...] = jnp.zeros_like(acc)
    source.prepare()

    def group(at, carry):
        source.group(at)
        products = []
        for inner in range(source.step):
            slot = at * source.step + inner
            place = source.index[slot]
            named = place < leading * trailing
            lead = jnp.where(named, place // trailing, leading)
            products.append(
                (lead, jnp.dot(source.blocks[slot], turned[place % trailing], preferred_element_type=F32))
            )
        for lead, product in products:
            acc[lead] += product
        return carry

    lax.fori_loop(0, source.blocks.shape[0] // source.step, group, 0)


def split_halves(core, read, targets, keep_ref, give_ref):
    half = keep_ref.shape[1]
    for at in range(targets):
        low, high = read(at, 0), read(at, half)
        keep_ref[at] = jnp.where(core == 0, low, high).astype(BF16)
        give_ref[at] = jnp.where(core == 0, high, low).astype(BF16)


def position(axis):
    return lax.axis_index(axis).astype(jnp.int32)


def core():
    return position("row") % 2


def pack_kernel(tokens_ref, cot_ref, mine_ref, held, sems):
    copies = [
        pltpu.make_async_copy(source, held.at[at], sems.at[at])
        for at, source in enumerate((tokens_ref, cot_ref))
    ]
    for copy in copies:
        copy.start()
    for copy in copies:
        copy.wait()
    mine_ref[...] = jnp.concatenate([held[0].astype(F32), held[1].astype(F32)]).astype(BF16)


def up_kernel(leading, trailing, index_hbm, blocks_hbm, *refs):
    parts = refs[:-9]
    tokens_ref, cot_ref, keep_ref, give_ref, acc = refs[-9:-4]
    source = Stream(index_hbm, blocks_hbm, *refs[-4:])
    rows = parts[0].shape[0] // 2
    for pair in range(len(parts) // 2):
        here = pl.ds(pair * 2 * rows, 2 * rows)
        for at in range(leading):
            lanes = pl.ds(at * BS, BS)
            first = parts[2 * pair][:, lanes].astype(F32)
            second = parts[2 * pair + 1][:, lanes].astype(F32)
            tokens_ref[at, here, :] = jnp.concatenate([first[:rows], second[:rows]]).astype(BF16)
            cot_ref[at, here, :] = jnp.concatenate([first[rows:], second[rows:]]).astype(BF16)
    accumulate(source, leading, trailing, tokens_ref, acc)
    half = keep_ref.shape[1]
    split_halves(core(), lambda at, low: acc[at, low : low + half, :], trailing, keep_ref, give_ref)


def act_kernel(
    leading, trailing, index_ref, blocks_ref, cot_ref, after_ref, keep_ref, give_ref, turned, acc
):
    accumulate_turned(Held(index_ref, blocks_ref, 56), leading, trailing, cot_ref, turned, acc)
    half = keep_ref.shape[1]

    def read(at, low):
        return acc[at].T[low : low + half]

    split_halves(core(), read, leading, keep_ref, give_ref)


def join_halves(core, own_ref, other_ref, whole_ref):
    half = own_ref.shape[1]
    for at in range(own_ref.shape[0]):
        own, other = own_ref[at], other_ref[at]
        whole_ref[at, :half, :] = jnp.where(core == 0, own, other)
        whole_ref[at, half:, :] = jnp.where(core == 0, other, own)


def gelu_kernel(own_ref, other_ref, hidden_ref, slope_ref):
    for at in range(own_ref.shape[0]):
        preact = own_ref[at].astype(F32) + other_ref[at].astype(F32)
        hidden_ref[at] = gelu_value(preact).astype(BF16)
        slope_ref[at] = gelu_slope(preact)


def slope_kernel(own_ref, other_ref, slope_ref, after_ref, grad_ref):
    for at in range(own_ref.shape[0]):
        act_grad = own_ref[at].astype(F32) + other_ref[at].astype(F32)
        grad_ref[at] = (act_grad * slope_ref[at]).astype(BF16)


def down_kernel(
    leading, trailing, index_ref, blocks_ref, own_ref, other_ref, hidden_ref, terms_ref, acc
):
    join_halves(core(), own_ref, other_ref, hidden_ref)
    accumulate(Held(index_ref, blocks_ref, 56), leading, trailing, hidden_ref, acc)
    for at in range(trailing):
        terms_ref[at] = acc[at].astype(BF16)


def relayed(bit):
    return bit >= 4 and bit % 2 == 1


def input_kernel(
    leading, trailing, index_ref, blocks_ref, own_ref, other_ref, out_terms_ref, grad_ref, relay_ref, *refs
):
    chunks, turned, acc = refs[:-2], refs[-2], refs[-1]
    join_halves(core(), own_ref, other_ref, grad_ref)
    accumulate_turned(Held(index_ref, blocks_ref, 56), leading, trailing, grad_ref, turned, acc)
    devices = relay_ref.shape[0] + len(chunks)
    rows = grad_ref.shape[1] // devices
    for at in range(leading):
        outs, grads = out_terms_ref[at].astype(F32), acc[at].T
        direct, relays = list(chunks), [relay_ref.at[slot] for slot in range(relay_ref.shape[0])]
        for bit in range(devices):
            mine = slice(bit * rows, (bit + 1) * rows)
            target = (relays if relayed(bit) else direct).pop(0)
            target[:, pl.ds(at * BS, BS)] = jnp.concatenate([outs[mine], grads[mine]]).astype(BF16)


def block_grads(leading, trailing, index_ref, left_ref, right_ref, out_ref, turned, held, sems):
    slots = index_ref.shape[0]
    step = divisor(slots, 56)

    def out_copy(at):
        here = pl.ds(at * step, step)
        return pltpu.make_async_copy(held.at[here], out_ref.at[here], sems.at[at])

    for at in range(leading):
        turned[at] = left_ref[at].T

    def group(at, carry):
        for inner in range(step):
            slot = at * step + inner
            place = index_ref[slot]
            lead = jnp.minimum(place // trailing, leading - 1)
            product = jnp.dot(turned[lead], right_ref[place % trailing], preferred_element_type=F32)
            held[slot] = jnp.where(place < leading * trailing, product, 0.0).astype(BF16)
        out_copy(at).start()
        return carry

    lax.fori_loop(0, slots // step, group, 0)
    return [out_copy(at) for at in range(slots // step)]


def grad_kernel(index_ref, left_ref, right_ref, out_ref, mark_ref, turned, held, sems):
    copies = block_grads(
        left_ref.shape[0], right_ref.shape[0], index_ref, left_ref, right_ref, out_ref, turned, held, sems
    )
    mark_ref[...] = jnp.zeros_like(mark_ref)
    for copy in copies:
        copy.wait()


def merge_kernel(count, *refs):
    relay_ref, ins, outs = refs[0], refs[2 : 2 + count], refs[2 + count :]
    slots = relay_ref.shape[0]
    for at in range(count):
        value = ins[at][...]
        if at >= count - slots:
            value = (value.astype(F32) + relay_ref[at - count + slots].astype(F32)).astype(BF16)
        outs[at][...] = value


def shards(tokens, up_blocks, up_index, down_blocks, down_index, out_cot):
    rows, width = tokens.shape
    col_devices, row_devices = lax.axis_size("col"), lax.axis_size("row")
    row_blocks = width // BS
    col_blocks = FF // (BS * col_devices)
    tok_count = rows * col_devices
    half = tok_count // 2
    slots = up_index.shape[2]
    up_weight = pltpu.with_memory_space_constraint(up_blocks[0, 0], pltpu.HBM)
    down_weight = down_blocks[0, 0]
    up_place = pltpu.with_memory_space_constraint(up_index[0, 0], pltpu.HBM)
    down_place = down_index[0, 0]
    cost = pl.CostEstimate(
        flops=2 * slots * BS * BS * tok_count, bytes_accessed=2 * slots * BS * BS, transcendentals=0
    )

    def swap(values, axis, bit):
        count = lax.axis_size(axis)
        return lax.ppermute(values, axis, [(at, at ^ bit) for at in range(count)])

    def call(body, name, outs, ins, scratch, *args, out_specs=None, **more):
        return pl.pallas_call(
            body,
            out_shape=outs,
            in_specs=ins,
            out_specs=out_specs or jax.tree.map(lambda _: VMEM, outs),
            scratch_shapes=scratch,
            compiler_params=params(),
            name=name,
            **more,
        )(*args)

    def shape(*dims, dtype=BF16):
        return jax.ShapeDtypeStruct(dims, dtype)

    long = pl.CostEstimate(flops=0, bytes_accessed=1 << 25, transcendentals=0)
    mine = call(
        pack_kernel,
        "pack",
        shape(2 * rows, width),
        [HBM] * 2,
        [pltpu.VMEM((2, rows, width), BF16), pltpu.SemaphoreType.DMA((2,))],
        pltpu.with_memory_space_constraint(tokens, pltpu.HBM),
        pltpu.with_memory_space_constraint(out_cot, pltpu.HBM),
        cost_estimate=long,
    )
    parts = {0: mine}
    for bit in sorted(range(1, col_devices), key=lambda bit: (bit < 4, bit % 2 if bit >= 4 else 0, bit)):
        parts[bit] = swap(parts[bit - 1], "col", 1) if relayed(bit) else swap(mine, "col", bit)
    parts = [parts[bit] for bit in range(col_devices)]

    tile_rows = shape(row_blocks, tok_count, BS)
    tile_cols = shape(col_blocks, tok_count, BS)
    half_cols = shape(col_blocks, half, BS)
    chunk = shape(2 * rows, width)
    acc_rows = pltpu.VMEM((row_blocks + 1, tok_count, BS), F32)
    acc_cols = pltpu.VMEM((col_blocks + 1, tok_count, BS), F32)
    acc_rows_turned = pltpu.VMEM((row_blocks + 1, BS, tok_count), F32)
    acc_cols_turned = pltpu.VMEM((col_blocks + 1, BS, tok_count), F32)
    rows_turned = pltpu.VMEM((row_blocks, BS, tok_count), BF16)
    cols_turned = pltpu.VMEM((col_blocks, BS, tok_count), BF16)
    ANY = pl.BlockSpec(memory_space=pl.ANY)

    def pair_sum(keep, give, cut=1):
        parts = [swap(part, "row", 1) for part in jnp.split(give, cut)]
        total = (keep.astype(F32) + jnp.concatenate(parts).astype(F32)).astype(BF16)
        bit = 2
        while 2 * bit < row_devices:
            total = (total.astype(F32) + swap(total, "row", bit).astype(F32)).astype(BF16)
            bit *= 2
        return total

    last = row_devices // 2
    features, cotangents, pre_keep, pre_give = call(
        functools.partial(up_kernel, row_blocks, col_blocks),
        "up",
        (tile_rows, tile_rows, half_cols, half_cols),
        [HBM, HBM] + [VMEM] * len(parts),
        [acc_cols] + Stream.scratch(slots, 28),
        up_place,
        up_weight,
        *parts,
        cost_estimate=cost,
    )
    pre_own = pair_sum(pre_keep, pre_give)
    pre_other = swap(pre_own, "row", last)

    act_keep, act_give = call(
        functools.partial(act_kernel, col_blocks, row_blocks),
        "act",
        (half_cols, half_cols),
        [SMEM, VMEM, VMEM, ANY],
        [rows_turned, acc_cols_turned],
        down_place,
        down_weight,
        cotangents,
        pre_own,
        cost_estimate=cost,
    )
    act_own = pair_sum(act_keep, act_give)
    act_other = swap(act_own, "row", last)

    hidden_own, slope = call(
        gelu_kernel,
        "gelu",
        (half_cols, shape(col_blocks, half, BS, dtype=F32)),
        [VMEM, VMEM],
        [],
        pre_own,
        pre_other,
    )
    hidden, out_terms = call(
        functools.partial(down_kernel, col_blocks, row_blocks),
        "down",
        (tile_cols, tile_rows),
        [SMEM, VMEM, VMEM, VMEM],
        [acc_rows],
        down_place,
        down_weight,
        hidden_own,
        swap(hidden_own, "row", 1),
        cost_estimate=cost,
    )

    def grads(name, index, left, right):
        return call(
            grad_kernel,
            name,
            (shape(slots, BS, BS), shape(8, BS, dtype=F32)),
            [SMEM, VMEM, VMEM],
            [
                pltpu.VMEM((left.shape[0], BS, tok_count), BF16),
                pltpu.VMEM((slots, BS, BS), BF16),
                pltpu.SemaphoreType.DMA((slots // divisor(slots, 56),)),
            ],
            index,
            left,
            right,
            out_specs=(HBM, VMEM),
            cost_estimate=cost,
        )

    down_grad, down_mark = grads("down_grad", down_place, hidden, cotangents)
    grad_own = call(
        slope_kernel, "slope", half_cols, [VMEM] * 4, [], act_own, act_other, slope, down_mark
    )
    by_way = [bit for bit in range(col_devices) if relayed(bit)]
    direct = [bit for bit in range(col_devices) if not relayed(bit)]
    pre_grad, relay, *chunks = call(
        functools.partial(input_kernel, row_blocks, col_blocks),
        "input",
        (tile_cols, shape(len(by_way), 2 * rows, width)) + (chunk,) * len(direct),
        [SMEM, VMEM, VMEM, VMEM, VMEM],
        [cols_turned, acc_rows_turned],
        up_index[0, 0],
        up_blocks[0, 0],
        grad_own,
        swap(grad_own, "row", 1),
        out_terms,
        cost_estimate=cost,
    )
    up_grad, up_mark = grads("up_grad", up_index[0, 0], features, pre_grad)
    later = [bit for bit in direct if bit not in (2,)]
    merged = call(
        functools.partial(merge_kernel, len(later)),
        "merge",
        (chunk,) * len(later),
        [VMEM] * (2 + len(later)),
        [],
        swap(relay, "col", 1),
        down_mark,
        *(chunks[direct.index(bit)] for bit in later),
    )
    chunks = dict(zip(direct, chunks)) | dict(zip(later, merged))
    total = chunks[0].astype(F32)
    for bit in sorted(direct[1:], key=lambda bit: -bit):
        total = total + swap(chunks[bit], "col", bit).astype(F32)
    total = total.astype(BF16)
    return total[:rows], total[rows:], up_grad[None, None], down_grad[None, None]


def solution(mesh):
    placed = (
        P("col", "row"),
        P("row", "col", None, None, None),
        P("row", "col", None),
        P("row", "col", None, None, None),
        P("row", "col", None),
        P("col", "row"),
    )
    return jax.shard_map(
        shards,
        mesh=mesh,
        in_specs=placed,
        out_specs=(
            P("col", "row"),
            P("col", "row"),
            P("row", "col", None, None, None),
            P("row", "col", None, None, None),
        ),
        check_vma=False,
    )
```

```python
import functools

import jax
import jax.numpy as jnp
from jax import lax
from jax.experimental import pallas as pl
from jax.experimental.pallas import tpu as pltpu
from jax.sharding import PartitionSpec as P

FF = 28672
BS = 128
COEF = 0.7978845608
CUBIC = 0.044715
F32 = jnp.float32
BF16 = jnp.bfloat16
VMEM = pl.BlockSpec(memory_space=pltpu.VMEM)
SMEM = pl.BlockSpec(memory_space=pltpu.SMEM)
HBM = pl.BlockSpec(memory_space=pltpu.HBM)


def gelu_value(values):
    inner = COEF * (values + CUBIC * values * values * values)
    return 0.5 * values * (1.0 + jnp.tanh(inner))


def gelu_slope(values):
    tangent = jnp.tanh(COEF * (values + CUBIC * values * values * values))
    return 0.5 * (1.0 + tangent) + 0.5 * values * (1.0 - tangent * tangent) * COEF * (
        1.0 + 3.0 * CUBIC * values * values
    )


def params(megabytes=24):
    return pltpu.CompilerParams(vmem_limit_bytes=megabytes << 20)


def divisor(count, most):
    return max(step for step in range(1, most + 1) if count % step == 0)


class Stream:
    def __init__(self, index_hbm, blocks_hbm, index_ref, blocks_ref, index_sem, sems):
        self.index, self.blocks = index_ref, blocks_ref
        self.index_copy = pltpu.make_async_copy(index_hbm, index_ref, index_sem)
        self.step = blocks_ref.shape[0] // sems.shape[0]
        self.copies = lambda at: pltpu.make_async_copy(
            blocks_hbm.at[pl.ds(at * self.step, self.step)],
            blocks_ref.at[pl.ds(at * self.step, self.step)],
            sems.at[at],
        )
        self.index_copy.start()
        for at in range(sems.shape[0]):
            self.copies(at).start()

    @staticmethod
    def scratch(slots, most):
        return [
            pltpu.SMEM((slots,), jnp.int32),
            pltpu.VMEM((slots, BS, BS), BF16),
            pltpu.SemaphoreType.DMA,
            pltpu.SemaphoreType.DMA((slots // divisor(slots, most),)),
        ]

    def prepare(self):
        self.index_copy.wait()

    def group(self, at):
        self.copies(at).wait()


class Held:
    def __init__(self, index_ref, blocks_ref, most):
        self.index, self.blocks = index_ref, blocks_ref
        self.step = divisor(blocks_ref.shape[0], most)

    def prepare(self):
        pass

    def group(self, at):
        pass


def accumulate(source, leading, trailing, operand_ref, acc):
    acc[...] = jnp.zeros_like(acc)
    source.prepare()

    def group(at, carry):
        source.group(at)
        products = []
        for inner in range(source.step):
            slot = at * source.step + inner
            place = source.index[slot]
            lead = jnp.minimum(place // trailing, leading - 1)
            trail = jnp.where(place < leading * trailing, place % trailing, trailing)
            products.append(
                (trail, jnp.dot(operand_ref[lead], source.blocks[slot], preferred_element_type=F32))
            )
        for trail, product in products:
            acc[trail] += product
        return carry

    lax.fori_loop(0, source.blocks.shape[0] // source.step, group, 0)


def accumulate_turned(source, leading, trailing, operand_ref, turned, acc):
    for at in range(trailing):
        turned[at] = operand_ref[at].T
    acc[...] = jnp.zeros_like(acc)
    source.prepare()

    def group(at, carry):
        source.group(at)
        products = []
        for inner in range(source.step):
            slot = at * source.step + inner
            place = source.index[slot]
            named = place < leading * trailing
            lead = jnp.where(named, place // trailing, leading)
            products.append(
                (lead, jnp.dot(source.blocks[slot], turned[place % trailing], preferred_element_type=F32))
            )
        for lead, product in products:
            acc[lead] += product
        return carry

    lax.fori_loop(0, source.blocks.shape[0] // source.step, group, 0)


def split_halves(core, read, targets, keep_ref, give_ref):
    half = keep_ref.shape[1]
    for at in range(targets):
        low, high = read(at, 0), read(at, half)
        keep_ref[at] = jnp.where(core == 0, low, high).astype(BF16)
        give_ref[at] = jnp.where(core == 0, high, low).astype(BF16)


def position(axis):
    return lax.axis_index(axis).astype(jnp.int32)


def core():
    return position("row") % 2


def pack_kernel(tokens_ref, cot_ref, mine_ref, held, sems):
    copies = [
        pltpu.make_async_copy(source, held.at[at], sems.at[at])
        for at, source in enumerate((tokens_ref, cot_ref))
    ]
    for copy in copies:
        copy.start()
    for copy in copies:
        copy.wait()
    mine_ref[...] = jnp.concatenate([held[0].astype(F32), held[1].astype(F32)]).astype(BF16)


def up_kernel(leading, trailing, index_hbm, blocks_hbm, *refs):
    parts = refs[:-9]
    tokens_ref, cot_ref, keep_ref, give_ref, acc = refs[-9:-4]
    source = Stream(index_hbm, blocks_hbm, *refs[-4:])
    rows = parts[0].shape[0] // 2
    for pair in range(len(parts) // 2):
        here = pl.ds(pair * 2 * rows, 2 * rows)
        for at in range(leading):
            lanes = pl.ds(at * BS, BS)
            first = parts[2 * pair][:, lanes].astype(F32)
            second = parts[2 * pair + 1][:, lanes].astype(F32)
            tokens_ref[at, here, :] = jnp.concatenate([first[:rows], second[:rows]]).astype(BF16)
            cot_ref[at, here, :] = jnp.concatenate([first[rows:], second[rows:]]).astype(BF16)
    accumulate(source, leading, trailing, tokens_ref, acc)
    half = keep_ref.shape[1]
    split_halves(core(), lambda at, low: acc[at, low : low + half, :], trailing, keep_ref, give_ref)


def act_kernel(
    leading, trailing, index_ref, blocks_ref, cot_ref, keep_ref, give_ref, turned, acc
):
    accumulate_turned(Held(index_ref, blocks_ref, 56), leading, trailing, cot_ref, turned, acc)
    half = keep_ref.shape[1]

    def read(at, low):
        return acc[at].T[low : low + half]

    split_halves(core(), read, leading, keep_ref, give_ref)


def join_halves(core, pieces, whole_ref):
    half = whole_ref.shape[1] // 2
    base = 0
    for own_ref, other_ref in pieces:
        for at in range(own_ref.shape[0]):
            own, other = own_ref[at], other_ref[at]
            whole_ref[base + at, :half, :] = jnp.where(core == 0, own, other)
            whole_ref[base + at, half:, :] = jnp.where(core == 0, other, own)
        base += own_ref.shape[0]


def add_kernel(keep_ref, other_ref, after_ref, out_ref):
    for at in range(keep_ref.shape[0]):
        out_ref[at] = (keep_ref[at].astype(F32) + other_ref[at].astype(F32)).astype(BF16)


def gelu_kernel(own_ref, other_ref, after_ref, slope_ref, *pieces):
    base = 0
    for hidden_ref in pieces:
        for at in range(hidden_ref.shape[0]):
            preact = own_ref[base + at].astype(F32) + other_ref[base + at].astype(F32)
            hidden_ref[at] = gelu_value(preact).astype(BF16)
            slope_ref[base + at] = gelu_slope(preact)
        base += hidden_ref.shape[0]


def slope_kernel(own_ref, other_ref, slope_ref, after_ref, grad_ref):
    for at in range(own_ref.shape[0]):
        act_grad = own_ref[at].astype(F32) + other_ref[at].astype(F32)
        grad_ref[at] = (act_grad * slope_ref[at]).astype(BF16)


def down_kernel(leading, trailing, index_ref, blocks_ref, *refs):
    pieces, (hidden_ref, terms_ref, acc) = refs[:-3], refs[-3:]
    join_halves(core(), list(zip(pieces[::2], pieces[1::2])), hidden_ref)
    accumulate(Held(index_ref, blocks_ref, 56), leading, trailing, hidden_ref, acc)
    for at in range(trailing):
        terms_ref[at] = acc[at].astype(BF16)


def relayed(bit):
    return bit >= 4 and bit % 2 == 1


def input_kernel(
    leading, trailing, index_ref, blocks_ref, own_ref, other_ref, out_terms_ref, grad_ref, relay_ref, *refs
):
    chunks, turned, acc = refs[:-2], refs[-2], refs[-1]
    join_halves(core(), [(own_ref, other_ref)], grad_ref)
    accumulate_turned(Held(index_ref, blocks_ref, 56), leading, trailing, grad_ref, turned, acc)
    devices = relay_ref.shape[0] + len(chunks)
    rows = grad_ref.shape[1] // devices
    for at in range(leading):
        outs, grads = out_terms_ref[at].astype(F32), acc[at].T
        direct, relays = list(chunks), [relay_ref.at[slot] for slot in range(relay_ref.shape[0])]
        for bit in range(devices):
            mine = slice(bit * rows, (bit + 1) * rows)
            target = (relays if relayed(bit) else direct).pop(0)
            target[:, pl.ds(at * BS, BS)] = jnp.concatenate([outs[mine], grads[mine]]).astype(BF16)


def block_grads(leading, trailing, index_ref, left_ref, right_ref, out_ref, turned, held, sems):
    slots = index_ref.shape[0]
    step = divisor(slots, 56)

    def out_copy(at):
        here = pl.ds(at * step, step)
        return pltpu.make_async_copy(held.at[here], out_ref.at[here], sems.at[at])

    for at in range(leading):
        turned[at] = left_ref[at].T

    def group(at, carry):
        for inner in range(step):
            slot = at * step + inner
            place = index_ref[slot]
            lead = jnp.minimum(place // trailing, leading - 1)
            product = jnp.dot(turned[lead], right_ref[place % trailing], preferred_element_type=F32)
            held[slot] = jnp.where(place < leading * trailing, product, 0.0).astype(BF16)
        out_copy(at).start()
        return carry

    lax.fori_loop(0, slots // step, group, 0)
    return [out_copy(at) for at in range(slots // step)]


def grad_kernel(index_ref, left_ref, right_ref, out_ref, mark_ref, turned, held, sems):
    copies = block_grads(
        left_ref.shape[0], right_ref.shape[0], index_ref, left_ref, right_ref, out_ref, turned, held, sems
    )
    mark_ref[...] = jnp.zeros_like(mark_ref)
    for copy in copies:
        copy.wait()


def merge_kernel(count, *refs):
    relay_ref, ins, outs = refs[0], refs[2 : 2 + count], refs[2 + count :]
    slots = relay_ref.shape[0]
    for at in range(count):
        value = ins[at][...]
        if at >= count - slots:
            value = (value.astype(F32) + relay_ref[at - count + slots].astype(F32)).astype(BF16)
        outs[at][...] = value


def shards(tokens, up_blocks, up_index, down_blocks, down_index, out_cot):
    rows, width = tokens.shape
    col_devices, row_devices = lax.axis_size("col"), lax.axis_size("row")
    row_blocks = width // BS
    col_blocks = FF // (BS * col_devices)
    tok_count = rows * col_devices
    half = tok_count // 2
    slots = up_index.shape[2]
    up_weight = pltpu.with_memory_space_constraint(up_blocks[0, 0], pltpu.HBM)
    down_weight = down_blocks[0, 0]
    up_place = pltpu.with_memory_space_constraint(up_index[0, 0], pltpu.HBM)
    down_place = down_index[0, 0]
    cost = pl.CostEstimate(
        flops=2 * slots * BS * BS * tok_count, bytes_accessed=2 * slots * BS * BS, transcendentals=0
    )

    def swap(values, axis, bit):
        count = lax.axis_size(axis)
        return lax.ppermute(values, axis, [(at, at ^ bit) for at in range(count)])

    def call(body, name, outs, ins, scratch, *args, out_specs=None, **more):
        return pl.pallas_call(
            body,
            out_shape=outs,
            in_specs=ins,
            out_specs=out_specs or jax.tree.map(lambda _: VMEM, outs),
            scratch_shapes=scratch,
            compiler_params=params(),
            name=name,
            **more,
        )(*args)

    def shape(*dims, dtype=BF16):
        return jax.ShapeDtypeStruct(dims, dtype)

    long = pl.CostEstimate(flops=0, bytes_accessed=1 << 25, transcendentals=0)
    mine = call(
        pack_kernel,
        "pack",
        shape(2 * rows, width),
        [HBM] * 2,
        [pltpu.VMEM((2, rows, width), BF16), pltpu.SemaphoreType.DMA((2,))],
        pltpu.with_memory_space_constraint(tokens, pltpu.HBM),
        pltpu.with_memory_space_constraint(out_cot, pltpu.HBM),
        cost_estimate=long,
    )
    parts = {0: mine}
    for bit in sorted(range(1, col_devices), key=lambda bit: (bit < 4, bit % 2 if bit >= 4 else 0, bit)):
        parts[bit] = swap(parts[bit - 1], "col", 1) if relayed(bit) else swap(mine, "col", bit)
    parts = [parts[bit] for bit in range(col_devices)]

    tile_rows = shape(row_blocks, tok_count, BS)
    tile_cols = shape(col_blocks, tok_count, BS)
    half_cols = shape(col_blocks, half, BS)
    chunk = shape(2 * rows, width)
    acc_rows = pltpu.VMEM((row_blocks + 1, tok_count, BS), F32)
    acc_cols = pltpu.VMEM((col_blocks + 1, tok_count, BS), F32)
    acc_rows_turned = pltpu.VMEM((row_blocks + 1, BS, tok_count), F32)
    acc_cols_turned = pltpu.VMEM((col_blocks + 1, BS, tok_count), F32)
    rows_turned = pltpu.VMEM((row_blocks, BS, tok_count), BF16)
    cols_turned = pltpu.VMEM((col_blocks, BS, tok_count), BF16)
    ANY = pl.BlockSpec(memory_space=pl.ANY)

    def pair_sum(keep, give, after):
        total = call(
            add_kernel, "add", half_cols, [VMEM, VMEM, ANY], [], keep, swap(give, "row", 1), after
        )
        bit = 2
        while 2 * bit < row_devices:
            total = (total.astype(F32) + swap(total, "row", bit).astype(F32)).astype(BF16)
            bit *= 2
        return total

    last = row_devices // 2
    features, cotangents, pre_keep, pre_give = call(
        functools.partial(up_kernel, row_blocks, col_blocks),
        "up",
        (tile_rows, tile_rows, half_cols, half_cols),
        [HBM, HBM] + [VMEM] * len(parts),
        [acc_cols] + Stream.scratch(slots, 28),
        up_place,
        up_weight,
        *parts,
        cost_estimate=cost,
    )
    act_keep, act_give = call(
        functools.partial(act_kernel, col_blocks, row_blocks),
        "act",
        (half_cols, half_cols),
        [SMEM, VMEM, VMEM],
        [rows_turned, acc_cols_turned],
        down_place,
        down_weight,
        cotangents,
        cost_estimate=cost,
    )
    pre_own = pair_sum(pre_keep, pre_give, act_keep)
    pre_other = swap(pre_own, "row", last)
    act_own = pair_sum(act_keep, act_give, act_keep)
    act_other = swap(act_own, "row", last)

    cut = (col_blocks + 1) // 2
    slope, *hidden_own = call(
        gelu_kernel,
        "gelu",
        (shape(col_blocks, half, BS, dtype=F32),)
        + tuple(shape(count, half, BS) for count in (cut, col_blocks - cut)),
        [VMEM, VMEM, ANY],
        [],
        pre_own,
        pre_other,
        act_own,
    )
    hidden, out_terms = call(
        functools.partial(down_kernel, col_blocks, row_blocks),
        "down",
        (tile_cols, tile_rows),
        [SMEM] + [VMEM] * (1 + 2 * len(hidden_own)),
        [acc_rows],
        down_place,
        down_weight,
        *(each for piece in hidden_own for each in (piece, swap(piece, "row", 1))),
        cost_estimate=cost,
    )

    def grads(name, index, left, right):
        return call(
            grad_kernel,
            name,
            (shape(slots, BS, BS), shape(8, BS, dtype=F32)),
            [SMEM, VMEM, VMEM],
            [
                pltpu.VMEM((left.shape[0], BS, tok_count), BF16),
                pltpu.VMEM((slots, BS, BS), BF16),
                pltpu.SemaphoreType.DMA((slots // divisor(slots, 56),)),
            ],
            index,
            left,
            right,
            out_specs=(HBM, VMEM),
            cost_estimate=cost,
        )

    down_grad, down_mark = grads("down_grad", down_place, hidden, cotangents)
    grad_own = call(
        slope_kernel, "slope", half_cols, [VMEM] * 3 + [ANY], [], act_own, act_other, slope, out_terms
    )
    by_way = [bit for bit in range(col_devices) if relayed(bit)]
    direct = [bit for bit in range(col_devices) if not relayed(bit)]
    pre_grad, relay, *chunks = call(
        functools.partial(input_kernel, row_blocks, col_blocks),
        "input",
        (tile_cols, shape(len(by_way), 2 * rows, width)) + (chunk,) * len(direct),
        [SMEM, VMEM, VMEM, VMEM, VMEM],
        [cols_turned, acc_rows_turned],
        up_index[0, 0],
        up_blocks[0, 0],
        grad_own,
        swap(grad_own, "row", 1),
        out_terms,
        cost_estimate=cost,
    )
    up_grad, up_mark = grads("up_grad", up_index[0, 0], features, pre_grad)
    later = [bit for bit in direct if bit not in (2,)]
    merged = call(
        functools.partial(merge_kernel, len(later)),
        "merge",
        (chunk,) * len(later),
        [VMEM] * (2 + len(later)),
        [],
        swap(relay, "col", 1),
        down_mark,
        *(chunks[direct.index(bit)] for bit in later),
    )
    chunks = dict(zip(direct, chunks)) | dict(zip(later, merged))
    total = chunks[0].astype(F32)
    for bit in sorted(direct[1:], key=lambda bit: -bit):
        total = total + swap(chunks[bit], "col", bit).astype(F32)
    total = total.astype(BF16)
    return total[:rows], total[rows:], up_grad[None, None], down_grad[None, None]


def solution(mesh):
    placed = (
        P("col", "row"),
        P("row", "col", None, None, None),
        P("row", "col", None),
        P("row", "col", None, None, None),
        P("row", "col", None),
        P("col", "row"),
    )
    return jax.shard_map(
        shards,
        mesh=mesh,
        in_specs=placed,
        out_specs=(
            P("col", "row"),
            P("col", "row"),
            P("row", "col", None, None, None),
            P("row", "col", None, None, None),
        ),
        check_vma=False,
    )
```

```python
import functools

import jax
import jax.numpy as jnp
from jax import lax
from jax.experimental import pallas as pl
from jax.experimental.pallas import tpu as pltpu
from jax.sharding import PartitionSpec as P

FF = 28672
BS = 128
COEF = 0.7978845608
CUBIC = 0.044715
F32 = jnp.float32
BF16 = jnp.bfloat16
VMEM = pl.BlockSpec(memory_space=pltpu.VMEM)
SMEM = pl.BlockSpec(memory_space=pltpu.SMEM)
HBM = pl.BlockSpec(memory_space=pltpu.HBM)


def gelu_value(values):
    inner = COEF * (values + CUBIC * values * values * values)
    return 0.5 * values * (1.0 + jnp.tanh(inner))


def gelu_slope(values):
    tangent = jnp.tanh(COEF * (values + CUBIC * values * values * values))
    return 0.5 * (1.0 + tangent) + 0.5 * values * (1.0 - tangent * tangent) * COEF * (
        1.0 + 3.0 * CUBIC * values * values
    )


def params(megabytes=24):
    return pltpu.CompilerParams(vmem_limit_bytes=megabytes << 20)


def divisor(count, most):
    return max(step for step in range(1, most + 1) if count % step == 0)


class Stream:
    def __init__(self, index_hbm, blocks_hbm, index_ref, blocks_ref, index_sem, sems):
        self.index, self.blocks = index_ref, blocks_ref
        self.index_copy = pltpu.make_async_copy(index_hbm, index_ref, index_sem)
        self.step = blocks_ref.shape[0] // sems.shape[0]
        self.copies = lambda at: pltpu.make_async_copy(
            blocks_hbm.at[pl.ds(at * self.step, self.step)],
            blocks_ref.at[pl.ds(at * self.step, self.step)],
            sems.at[at],
        )
        self.index_copy.start()
        for at in range(sems.shape[0]):
            self.copies(at).start()

    @staticmethod
    def scratch(slots, most):
        return [
            pltpu.SMEM((slots,), jnp.int32),
            pltpu.VMEM((slots, BS, BS), BF16),
            pltpu.SemaphoreType.DMA,
            pltpu.SemaphoreType.DMA((slots // divisor(slots, most),)),
        ]

    def prepare(self):
        self.index_copy.wait()

    def group(self, at):
        self.copies(at).wait()


class Held:
    def __init__(self, index_ref, blocks_ref, most):
        self.index, self.blocks = index_ref, blocks_ref
        self.step = divisor(blocks_ref.shape[0], most)

    def prepare(self):
        pass

    def group(self, at):
        pass


def accumulate(source, leading, trailing, operand_ref, acc):
    acc[...] = jnp.zeros_like(acc)
    source.prepare()

    def group(at, carry):
        source.group(at)
        products = []
        for inner in range(source.step):
            slot = at * source.step + inner
            place = source.index[slot]
            lead = jnp.minimum(place // trailing, leading - 1)
            trail = jnp.where(place < leading * trailing, place % trailing, trailing)
            products.append(
                (trail, jnp.dot(operand_ref[lead], source.blocks[slot], preferred_element_type=F32))
            )
        for trail, product in products:
            acc[trail] += product
        return carry

    lax.fori_loop(0, source.blocks.shape[0] // source.step, group, 0)


def accumulate_turned(source, leading, trailing, operand_ref, turned, acc):
    for at in range(trailing):
        turned[at] = operand_ref[at].T
    acc[...] = jnp.zeros_like(acc)
    source.prepare()

    def group(at, carry):
        source.group(at)
        products = []
        for inner in range(source.step):
            slot = at * source.step + inner
            place = source.index[slot]
            named = place < leading * trailing
            lead = jnp.where(named, place // trailing, leading)
            products.append(
                (lead, jnp.dot(source.blocks[slot], turned[place % trailing], preferred_element_type=F32))
            )
        for lead, product in products:
            acc[lead] += product
        return carry

    lax.fori_loop(0, source.blocks.shape[0] // source.step, group, 0)


def split_halves(core, read, targets, keep_ref, gives):
    half = keep_ref.shape[1]
    places = [(give_ref, at) for give_ref in gives for at in range(give_ref.shape[0])]
    for at, (give_ref, place) in zip(range(targets), places):
        low, high = read(at, 0), read(at, half)
        keep_ref[at] = jnp.where(core == 0, low, high).astype(BF16)
        give_ref[place] = jnp.where(core == 0, high, low).astype(BF16)


def position(axis):
    return lax.axis_index(axis).astype(jnp.int32)


def core():
    return position("row") % 2


def pack_kernel(tokens_ref, cot_ref, mine_ref, held, sems):
    copies = [
        pltpu.make_async_copy(source, held.at[at], sems.at[at])
        for at, source in enumerate((tokens_ref, cot_ref))
    ]
    for copy in copies:
        copy.start()
    for copy in copies:
        copy.wait()
    mine_ref[...] = jnp.concatenate([held[0].astype(F32), held[1].astype(F32)]).astype(BF16)


def fetch_kernel(index_hbm, blocks_hbm, after_ref, index_ref, blocks_ref, sems):
    copies = [
        pltpu.make_async_copy(source, target, sems.at[at])
        for at, (source, target) in enumerate(((index_hbm, index_ref), (blocks_hbm, blocks_ref)))
    ]
    for copy in copies:
        copy.start()
    for copy in copies:
        copy.wait()


def up_kernel(leading, trailing, index_ref, blocks_ref, *refs):
    parts = refs[:-5]
    tokens_ref, cot_ref, keep_ref, give_ref, acc = refs[-5:]
    source = Held(index_ref, blocks_ref, 56)
    rows = parts[0].shape[0] // 2
    for pair in range(len(parts) // 2):
        here = pl.ds(pair * 2 * rows, 2 * rows)
        for at in range(leading):
            lanes = pl.ds(at * BS, BS)
            first = parts[2 * pair][:, lanes].astype(F32)
            second = parts[2 * pair + 1][:, lanes].astype(F32)
            tokens_ref[at, here, :] = jnp.concatenate([first[:rows], second[:rows]]).astype(BF16)
            cot_ref[at, here, :] = jnp.concatenate([first[rows:], second[rows:]]).astype(BF16)
    accumulate(source, leading, trailing, tokens_ref, acc)
    half = keep_ref.shape[1]
    split_halves(core(), lambda at, low: acc[at, low : low + half, :], trailing, keep_ref, [give_ref])


def act_kernel(
    leading, trailing, index_ref, blocks_ref, cot_ref, keep_ref, *refs
):
    gives, (turned, acc) = refs[:-2], refs[-2:]
    accumulate_turned(Held(index_ref, blocks_ref, 56), leading, trailing, cot_ref, turned, acc)
    half = keep_ref.shape[1]

    def read(at, low):
        return acc[at].T[low : low + half]

    split_halves(core(), read, leading, keep_ref, gives)


def join_halves(core, pieces, whole_ref):
    half = whole_ref.shape[1] // 2
    base = 0
    for own_ref, other_ref in pieces:
        for at in range(own_ref.shape[0]):
            own, other = own_ref[at], other_ref[at]
            whole_ref[base + at, :half, :] = jnp.where(core == 0, own, other)
            whole_ref[base + at, half:, :] = jnp.where(core == 0, other, own)
        base += own_ref.shape[0]


def add_kernel(keep_ref, after_ref, *refs):
    others, out_ref = refs[:-1], refs[-1]
    base = 0
    for other_ref in others:
        for at in range(other_ref.shape[0]):
            out_ref[base + at] = (keep_ref[base + at].astype(F32) + other_ref[at].astype(F32)).astype(BF16)
        base += other_ref.shape[0]


def gelu_kernel(own_ref, other_ref, after_ref, slope_ref, *pieces):
    base = 0
    for hidden_ref in pieces:
        for at in range(hidden_ref.shape[0]):
            preact = own_ref[base + at].astype(F32) + other_ref[base + at].astype(F32)
            hidden_ref[at] = gelu_value(preact).astype(BF16)
            slope_ref[base + at] = gelu_slope(preact)
        base += hidden_ref.shape[0]


def slope_kernel(own_ref, other_ref, slope_ref, after_ref, grad_ref):
    for at in range(own_ref.shape[0]):
        act_grad = own_ref[at].astype(F32) + other_ref[at].astype(F32)
        grad_ref[at] = (act_grad * slope_ref[at]).astype(BF16)


def down_kernel(leading, trailing, index_ref, blocks_ref, *refs):
    pieces, (hidden_ref, terms_ref, acc) = refs[:-3], refs[-3:]
    join_halves(core(), list(zip(pieces[::2], pieces[1::2])), hidden_ref)
    accumulate(Held(index_ref, blocks_ref, 56), leading, trailing, hidden_ref, acc)
    for at in range(trailing):
        terms_ref[at] = acc[at].astype(BF16)


def relayed(bit):
    return bit >= 4 and bit % 2 == 1


def input_kernel(
    leading, trailing, index_ref, blocks_ref, own_ref, other_ref, out_terms_ref, grad_ref, relay_ref, *refs
):
    chunks, turned, acc = refs[:-2], refs[-2], refs[-1]
    join_halves(core(), [(own_ref, other_ref)], grad_ref)
    accumulate_turned(Held(index_ref, blocks_ref, 56), leading, trailing, grad_ref, turned, acc)
    devices = relay_ref.shape[0] + len(chunks)
    rows = grad_ref.shape[1] // devices
    for at in range(leading):
        outs, grads = out_terms_ref[at].astype(F32), acc[at].T
        direct, relays = list(chunks), [relay_ref.at[slot] for slot in range(relay_ref.shape[0])]
        for bit in range(devices):
            mine = slice(bit * rows, (bit + 1) * rows)
            target = (relays if relayed(bit) else direct).pop(0)
            target[:, pl.ds(at * BS, BS)] = jnp.concatenate([outs[mine], grads[mine]]).astype(BF16)


def turn_kernel(*refs):
    count = len(refs) // 2
    for source, target in zip(refs[:count], refs[count:]):
        for at in range(source.shape[0]):
            target[at] = source[at].T


def grad_kernel(index_ref, turned_ref, right_ref, out_ref, mark_ref, held, sems):
    leading, trailing = turned_ref.shape[0], right_ref.shape[0]
    slots = index_ref.shape[0]
    step = divisor(slots, 56)

    def out_copy(at):
        here = pl.ds(at * step, step)
        return pltpu.make_async_copy(held.at[here], out_ref.at[here], sems.at[at])

    def group(at, carry):
        for inner in range(step):
            slot = at * step + inner
            place = index_ref[slot]
            lead = jnp.minimum(place // trailing, leading - 1)
            product = jnp.dot(turned_ref[lead], right_ref[place % trailing], preferred_element_type=F32)
            held[slot] = jnp.where(place < leading * trailing, product, 0.0).astype(BF16)
        out_copy(at).start()
        return carry

    lax.fori_loop(0, slots // step, group, 0)
    mark_ref[...] = jnp.zeros_like(mark_ref)
    for at in range(slots // step):
        out_copy(at).wait()


def merge_kernel(count, *refs):
    relay_ref, ins, outs = refs[0], refs[2 : 2 + count], refs[2 + count :]
    slots = relay_ref.shape[0]
    for at in range(count):
        value = ins[at][...]
        if at >= count - slots:
            value = (value.astype(F32) + relay_ref[at - count + slots].astype(F32)).astype(BF16)
        outs[at][...] = value


def shards(tokens, up_blocks, up_index, down_blocks, down_index, out_cot):
    rows, width = tokens.shape
    col_devices, row_devices = lax.axis_size("col"), lax.axis_size("row")
    row_blocks = width // BS
    col_blocks = FF // (BS * col_devices)
    tok_count = rows * col_devices
    half = tok_count // 2
    slots = up_index.shape[2]
    up_weight = pltpu.with_memory_space_constraint(up_blocks[0, 0], pltpu.HBM)
    down_weight = down_blocks[0, 0]
    up_place = pltpu.with_memory_space_constraint(up_index[0, 0], pltpu.HBM)
    down_place = down_index[0, 0]
    cost = pl.CostEstimate(
        flops=2 * slots * BS * BS * tok_count, bytes_accessed=2 * slots * BS * BS, transcendentals=0
    )

    def swap(values, axis, bit):
        count = lax.axis_size(axis)
        return lax.ppermute(values, axis, [(at, at ^ bit) for at in range(count)])

    def call(body, name, outs, ins, scratch, *args, out_specs=None, **more):
        return pl.pallas_call(
            body,
            out_shape=outs,
            in_specs=ins,
            out_specs=out_specs or jax.tree.map(lambda _: VMEM, outs),
            scratch_shapes=scratch,
            compiler_params=params(),
            name=name,
            **more,
        )(*args)

    def shape(*dims, dtype=BF16):
        return jax.ShapeDtypeStruct(dims, dtype)

    long = pl.CostEstimate(flops=0, bytes_accessed=1 << 25, transcendentals=0)
    mine = call(
        pack_kernel,
        "pack",
        shape(2 * rows, width),
        [HBM] * 2,
        [pltpu.VMEM((2, rows, width), BF16), pltpu.SemaphoreType.DMA((2,))],
        pltpu.with_memory_space_constraint(tokens, pltpu.HBM),
        pltpu.with_memory_space_constraint(out_cot, pltpu.HBM),
        cost_estimate=long,
    )
    parts = {0: mine}
    for bit in sorted(range(1, col_devices), key=lambda bit: (bit < 4, bit % 2 if bit >= 4 else 0, bit)):
        parts[bit] = swap(parts[bit - 1], "col", 1) if relayed(bit) else swap(mine, "col", bit)
    parts = [parts[bit] for bit in range(col_devices)]

    tile_rows = shape(row_blocks, tok_count, BS)
    tile_cols = shape(col_blocks, tok_count, BS)
    half_cols = shape(col_blocks, half, BS)
    chunk = shape(2 * rows, width)
    acc_rows = pltpu.VMEM((row_blocks + 1, tok_count, BS), F32)
    acc_cols = pltpu.VMEM((col_blocks + 1, tok_count, BS), F32)
    acc_rows_turned = pltpu.VMEM((row_blocks + 1, BS, tok_count), F32)
    acc_cols_turned = pltpu.VMEM((col_blocks + 1, BS, tok_count), F32)
    rows_turned = pltpu.VMEM((row_blocks, BS, tok_count), BF16)
    cols_turned = pltpu.VMEM((col_blocks, BS, tok_count), BF16)
    ANY = pl.BlockSpec(memory_space=pl.ANY)

    def pair_sum(keep, gives, after):
        others = [swap(give, "row", 1) for give in gives]
        total = call(
            add_kernel, "add", half_cols, [VMEM, ANY] + [VMEM] * len(others), [], keep, after, *others
        )
        bit = 2
        while 2 * bit < row_devices:
            total = (total.astype(F32) + swap(total, "row", bit).astype(F32)).astype(BF16)
            bit *= 2
        return total

    last = row_devices // 2
    up_place, up_weight = call(
        fetch_kernel,
        "fetch",
        (shape(slots, dtype=jnp.int32), shape(slots, BS, BS)),
        [HBM, HBM, VMEM],
        [pltpu.SemaphoreType.DMA((2,))],
        up_place,
        up_weight,
        parts[4 if col_devices > 4 else -1],
        out_specs=(SMEM, VMEM),
        cost_estimate=cost,
    )
    features, cotangents, pre_keep, pre_give = call(
        functools.partial(up_kernel, row_blocks, col_blocks),
        "up",
        (tile_rows, tile_rows, half_cols, half_cols),
        [SMEM] + [VMEM] * (1 + len(parts)),
        [acc_cols],
        up_place,
        up_weight,
        *parts,
        cost_estimate=cost,
    )
    pieces = 2
    bounds = [col_blocks * at // pieces for at in range(pieces + 1)]
    act_keep, *act_gives = call(
        functools.partial(act_kernel, col_blocks, row_blocks),
        "act",
        (half_cols,) + tuple(shape(b - a, half, BS) for a, b in zip(bounds, bounds[1:])),
        [SMEM, VMEM, VMEM],
        [rows_turned, acc_cols_turned],
        down_place,
        down_weight,
        cotangents,
        cost_estimate=cost,
    )
    pre_own = pair_sum(pre_keep, [pre_give], pre_keep)
    pre_other = swap(pre_own, "row", last)
    act_own = pair_sum(act_keep, act_gives, act_keep)
    act_other = swap(act_own, "row", last)

    cut = (col_blocks + 1) // 2
    slope, *hidden_own = call(
        gelu_kernel,
        "gelu",
        (shape(col_blocks, half, BS, dtype=F32),)
        + tuple(shape(count, half, BS) for count in (cut, col_blocks - cut)),
        [VMEM, VMEM, ANY],
        [],
        pre_own,
        pre_other,
        act_own,
    )
    hidden, out_terms = call(
        functools.partial(down_kernel, col_blocks, row_blocks),
        "down",
        (tile_cols, tile_rows),
        [SMEM] + [VMEM] * (1 + 2 * len(hidden_own)),
        [acc_rows],
        down_place,
        down_weight,
        *(each for piece in hidden_own for each in (piece, swap(piece, "row", 1))),
        cost_estimate=cost,
    )

    def grads(name, index, turned, right):
        return call(
            grad_kernel,
            name,
            (shape(slots, BS, BS), shape(8, BS, dtype=F32)),
            [SMEM, VMEM, VMEM],
            [
                pltpu.VMEM((slots, BS, BS), BF16),
                pltpu.SemaphoreType.DMA((slots // divisor(slots, 56),)),
            ],
            index,
            turned,
            right,
            out_specs=(HBM, VMEM),
            cost_estimate=cost,
        )

    turned_hidden, turned_features = call(
        turn_kernel,
        "turn",
        (shape(col_blocks, BS, tok_count), shape(row_blocks, BS, tok_count)),
        [VMEM] * 2,
        [],
        hidden,
        features,
    )
    down_grad, down_mark = grads("down_grad", down_place, turned_hidden, cotangents)
    grad_own = call(
        slope_kernel, "slope", half_cols, [VMEM] * 3 + [ANY], [], act_own, act_other, slope, turned_features
    )
    by_way = [bit for bit in range(col_devices) if relayed(bit)]
    direct = [bit for bit in range(col_devices) if not relayed(bit)]
    pre_grad, relay, *chunks = call(
        functools.partial(input_kernel, row_blocks, col_blocks),
        "input",
        (tile_cols, shape(len(by_way), 2 * rows, width)) + (chunk,) * len(direct),
        [SMEM, VMEM, VMEM, VMEM, VMEM],
        [cols_turned, acc_rows_turned],
        up_place,
        up_weight,
        grad_own,
        swap(grad_own, "row", 1),
        out_terms,
        cost_estimate=cost,
    )
    up_grad, up_mark = grads("up_grad", up_place, turned_features, pre_grad)
    later = [bit for bit in direct if bit not in (2,)]
    merged = call(
        functools.partial(merge_kernel, len(later)),
        "merge",
        (chunk,) * len(later),
        [VMEM] * (2 + len(later)),
        [],
        swap(relay, "col", 1),
        down_mark,
        *(chunks[direct.index(bit)] for bit in later),
    )
    chunks = dict(zip(direct, chunks)) | dict(zip(later, merged))
    total = chunks[0].astype(F32)
    for bit in sorted(direct[1:], key=lambda bit: -bit):
        total = total + swap(chunks[bit], "col", bit).astype(F32)
    total = total.astype(BF16)
    return total[:rows], total[rows:], up_grad[None, None], down_grad[None, None]


def solution(mesh):
    placed = (
        P("col", "row"),
        P("row", "col", None, None, None),
        P("row", "col", None),
        P("row", "col", None, None, None),
        P("row", "col", None),
        P("col", "row"),
    )
    return jax.shard_map(
        shards,
        mesh=mesh,
        in_specs=placed,
        out_specs=(
            P("col", "row"),
            P("col", "row"),
            P("row", "col", None, None, None),
            P("row", "col", None, None, None),
        ),
        check_vma=False,
    )
```

```python
import functools

import jax
import jax.numpy as jnp
from jax import lax
from jax.experimental import pallas as pl
from jax.experimental.pallas import tpu as pltpu
from jax.sharding import PartitionSpec as P

FF = 28672
BS = 128
COEF = 0.7978845608
CUBIC = 0.044715
F32 = jnp.float32
BF16 = jnp.bfloat16
VMEM = pl.BlockSpec(memory_space=pltpu.VMEM)
SMEM = pl.BlockSpec(memory_space=pltpu.SMEM)
HBM = pl.BlockSpec(memory_space=pltpu.HBM)


def gelu_value(values):
    inner = COEF * (values + CUBIC * values * values * values)
    return 0.5 * values * (1.0 + jnp.tanh(inner))


def gelu_slope(values):
    tangent = jnp.tanh(COEF * (values + CUBIC * values * values * values))
    return 0.5 * (1.0 + tangent) + 0.5 * values * (1.0 - tangent * tangent) * COEF * (
        1.0 + 3.0 * CUBIC * values * values
    )


def params(megabytes=24):
    return pltpu.CompilerParams(vmem_limit_bytes=megabytes << 20)


def divisor(count, most):
    return max(step for step in range(1, most + 1) if count % step == 0)


class Stream:
    def __init__(self, index_hbm, blocks_hbm, index_ref, blocks_ref, index_sem, sems):
        self.index, self.blocks = index_ref, blocks_ref
        self.index_copy = pltpu.make_async_copy(index_hbm, index_ref, index_sem)
        self.step = blocks_ref.shape[0] // sems.shape[0]
        self.copies = lambda at: pltpu.make_async_copy(
            blocks_hbm.at[pl.ds(at * self.step, self.step)],
            blocks_ref.at[pl.ds(at * self.step, self.step)],
            sems.at[at],
        )
        self.index_copy.start()
        for at in range(sems.shape[0]):
            self.copies(at).start()

    @staticmethod
    def scratch(slots, most):
        return [
            pltpu.SMEM((slots,), jnp.int32),
            pltpu.VMEM((slots, BS, BS), BF16),
            pltpu.SemaphoreType.DMA,
            pltpu.SemaphoreType.DMA((slots // divisor(slots, most),)),
        ]

    def prepare(self):
        self.index_copy.wait()

    def group(self, at):
        self.copies(at).wait()


class Held:
    def __init__(self, index_ref, blocks_ref, most):
        self.index, self.blocks = index_ref, blocks_ref
        self.step = divisor(blocks_ref.shape[0], most)

    def prepare(self):
        pass

    def group(self, at):
        pass


def accumulate(source, leading, trailing, operand_ref, acc):
    acc[...] = jnp.zeros_like(acc)
    source.prepare()

    def group(at, carry):
        source.group(at)
        products = []
        for inner in range(source.step):
            slot = at * source.step + inner
            place = source.index[slot]
            lead = jnp.minimum(place // trailing, leading - 1)
            trail = jnp.where(place < leading * trailing, place % trailing, trailing)
            products.append(
                (trail, jnp.dot(operand_ref[lead], source.blocks[slot], preferred_element_type=F32))
            )
        for trail, product in products:
            acc[trail] += product
        return carry

    lax.fori_loop(0, source.blocks.shape[0] // source.step, group, 0)


def accumulate_turned(source, leading, trailing, operand_ref, turned, acc):
    for at in range(trailing):
        turned[at] = operand_ref[at].T
    acc[...] = jnp.zeros_like(acc)
    source.prepare()

    def group(at, carry):
        source.group(at)
        products = []
        for inner in range(source.step):
            slot = at * source.step + inner
            place = source.index[slot]
            named = place < leading * trailing
            lead = jnp.where(named, place // trailing, leading)
            products.append(
                (lead, jnp.dot(source.blocks[slot], turned[place % trailing], preferred_element_type=F32))
            )
        for lead, product in products:
            acc[lead] += product
        return carry

    lax.fori_loop(0, source.blocks.shape[0] // source.step, group, 0)


def split_halves(core, read, targets, keep_ref, gives):
    half = keep_ref.shape[1]
    places = [(give_ref, at) for give_ref in gives for at in range(give_ref.shape[0])]
    for at, (give_ref, place) in zip(range(targets), places):
        low, high = read(at, 0), read(at, half)
        keep_ref[at] = jnp.where(core == 0, low, high).astype(BF16)
        give_ref[place] = jnp.where(core == 0, high, low).astype(BF16)


def position(axis):
    return lax.axis_index(axis).astype(jnp.int32)


def core():
    return position("row") % 2


def pack_kernel(tokens_ref, cot_ref, mine_ref, held, sems):
    copies = [
        pltpu.make_async_copy(source, held.at[at], sems.at[at])
        for at, source in enumerate((tokens_ref, cot_ref))
    ]
    for copy in copies:
        copy.start()
    for copy in copies:
        copy.wait()
    mine_ref[...] = jnp.concatenate([held[0].astype(F32), held[1].astype(F32)]).astype(BF16)


def fetch_kernel(index_hbm, blocks_hbm, after_ref, index_ref, blocks_ref, sems):
    copies = [
        pltpu.make_async_copy(source, target, sems.at[at])
        for at, (source, target) in enumerate(((index_hbm, index_ref), (blocks_hbm, blocks_ref)))
    ]
    for copy in copies:
        copy.start()
    for copy in copies:
        copy.wait()


def up_kernel(leading, trailing, index_ref, blocks_ref, *refs):
    parts = refs[:-5]
    tokens_ref, cot_ref, keep_ref, give_ref, acc = refs[-5:]
    source = Held(index_ref, blocks_ref, 112)
    rows = parts[0].shape[0] // 2
    for pair in range(len(parts) // 2):
        here = pl.ds(pair * 2 * rows, 2 * rows)
        for at in range(leading):
            lanes = pl.ds(at * BS, BS)
            first = parts[2 * pair][:, lanes].astype(F32)
            second = parts[2 * pair + 1][:, lanes].astype(F32)
            tokens_ref[at, here, :] = jnp.concatenate([first[:rows], second[:rows]]).astype(BF16)
            cot_ref[at, here, :] = jnp.concatenate([first[rows:], second[rows:]]).astype(BF16)
    accumulate(source, leading, trailing, tokens_ref, acc)
    half = keep_ref.shape[1]
    split_halves(core(), lambda at, low: acc[at, low : low + half, :], trailing, keep_ref, [give_ref])


def act_kernel(
    leading, trailing, index_ref, blocks_ref, cot_ref, keep_ref, *refs
):
    gives, (turned, acc) = refs[:-2], refs[-2:]
    accumulate_turned(Held(index_ref, blocks_ref, 112), leading, trailing, cot_ref, turned, acc)
    half = keep_ref.shape[1]

    def read(at, low):
        return acc[at].T[low : low + half]

    split_halves(core(), read, leading, keep_ref, gives)


def join_halves(core, pieces, whole_ref):
    half = whole_ref.shape[1] // 2
    base = 0
    for own_ref, other_ref in pieces:
        for at in range(own_ref.shape[0]):
            own, other = own_ref[at], other_ref[at]
            whole_ref[base + at, :half, :] = jnp.where(core == 0, own, other)
            whole_ref[base + at, half:, :] = jnp.where(core == 0, other, own)
        base += own_ref.shape[0]


def add_kernel(keep_ref, after_ref, *refs):
    others, out_ref = refs[:-1], refs[-1]
    base = 0
    for other_ref in others:
        for at in range(other_ref.shape[0]):
            out_ref[base + at] = (keep_ref[base + at].astype(F32) + other_ref[at].astype(F32)).astype(BF16)
        base += other_ref.shape[0]


def gelu_kernel(own_ref, other_ref, after_ref, slope_ref, *pieces):
    base = 0
    for hidden_ref in pieces:
        for at in range(hidden_ref.shape[0]):
            preact = own_ref[base + at].astype(F32) + other_ref[base + at].astype(F32)
            hidden_ref[at] = gelu_value(preact).astype(BF16)
            slope_ref[base + at] = gelu_slope(preact)
        base += hidden_ref.shape[0]


def slope_kernel(own_ref, other_ref, slope_ref, after_ref, grad_ref):
    for at in range(own_ref.shape[0]):
        act_grad = own_ref[at].astype(F32) + other_ref[at].astype(F32)
        grad_ref[at] = (act_grad * slope_ref[at]).astype(BF16)


def down_kernel(leading, trailing, index_ref, blocks_ref, *refs):
    pieces, (hidden_ref, terms_ref, acc) = refs[:-3], refs[-3:]
    join_halves(core(), list(zip(pieces[::2], pieces[1::2])), hidden_ref)
    accumulate(Held(index_ref, blocks_ref, 112), leading, trailing, hidden_ref, acc)
    for at in range(trailing):
        terms_ref[at] = acc[at].astype(BF16)


def relayed(bit):
    return bit >= 4 and bit % 2 == 1


def input_kernel(
    leading, trailing, index_ref, blocks_ref, own_ref, other_ref, out_terms_ref, grad_ref, relay_ref, *refs
):
    chunks, turned, acc = refs[:-2], refs[-2], refs[-1]
    join_halves(core(), [(own_ref, other_ref)], grad_ref)
    accumulate_turned(Held(index_ref, blocks_ref, 112), leading, trailing, grad_ref, turned, acc)
    devices = relay_ref.shape[0] + len(chunks)
    rows = grad_ref.shape[1] // devices
    for at in range(leading):
        outs, grads = out_terms_ref[at].astype(F32), acc[at].T
        direct, relays = list(chunks), [relay_ref.at[slot] for slot in range(relay_ref.shape[0])]
        for bit in range(devices):
            mine = slice(bit * rows, (bit + 1) * rows)
            target = (relays if relayed(bit) else direct).pop(0)
            target[:, pl.ds(at * BS, BS)] = jnp.concatenate([outs[mine], grads[mine]]).astype(BF16)


def turn_kernel(*refs):
    count = len(refs) // 2
    for source, target in zip(refs[:count], refs[count:]):
        for at in range(source.shape[0]):
            target[at] = source[at].T


def grad_kernel(index_ref, turned_ref, right_ref, out_ref, mark_ref, held, sems):
    leading, trailing = turned_ref.shape[0], right_ref.shape[0]
    slots = index_ref.shape[0]
    step = divisor(slots, 56)

    def out_copy(at):
        here = pl.ds(at * step, step)
        return pltpu.make_async_copy(held.at[here], out_ref.at[here], sems.at[at])

    def group(at, carry):
        for inner in range(step):
            slot = at * step + inner
            place = index_ref[slot]
            lead = jnp.minimum(place // trailing, leading - 1)
            product = jnp.dot(turned_ref[lead], right_ref[place % trailing], preferred_element_type=F32)
            held[slot] = jnp.where(place < leading * trailing, product, 0.0).astype(BF16)
        out_copy(at).start()
        return carry

    lax.fori_loop(0, slots // step, group, 0)
    mark_ref[...] = jnp.zeros_like(mark_ref)
    for at in range(slots // step):
        out_copy(at).wait()


def merge_kernel(count, *refs):
    relay_ref, ins, outs = refs[0], refs[2 : 2 + count], refs[2 + count :]
    slots = relay_ref.shape[0]
    for at in range(count):
        value = ins[at][...]
        if at >= count - slots:
            value = (value.astype(F32) + relay_ref[at - count + slots].astype(F32)).astype(BF16)
        outs[at][...] = value


def shards(tokens, up_blocks, up_index, down_blocks, down_index, out_cot):
    rows, width = tokens.shape
    col_devices, row_devices = lax.axis_size("col"), lax.axis_size("row")
    row_blocks = width // BS
    col_blocks = FF // (BS * col_devices)
    tok_count = rows * col_devices
    half = tok_count // 2
    slots = up_index.shape[2]
    up_weight = pltpu.with_memory_space_constraint(up_blocks[0, 0], pltpu.HBM)
    down_weight = down_blocks[0, 0]
    up_place = pltpu.with_memory_space_constraint(up_index[0, 0], pltpu.HBM)
    down_place = down_index[0, 0]
    cost = pl.CostEstimate(
        flops=2 * slots * BS * BS * tok_count, bytes_accessed=2 * slots * BS * BS, transcendentals=0
    )

    def swap(values, axis, bit):
        count = lax.axis_size(axis)
        return lax.ppermute(values, axis, [(at, at ^ bit) for at in range(count)])

    def call(body, name, outs, ins, scratch, *args, out_specs=None, **more):
        return pl.pallas_call(
            body,
            out_shape=outs,
            in_specs=ins,
            out_specs=out_specs or jax.tree.map(lambda _: VMEM, outs),
            scratch_shapes=scratch,
            compiler_params=params(),
            name=name,
            **more,
        )(*args)

    def shape(*dims, dtype=BF16):
        return jax.ShapeDtypeStruct(dims, dtype)

    long = pl.CostEstimate(flops=0, bytes_accessed=1 << 25, transcendentals=0)
    mine = call(
        pack_kernel,
        "pack",
        shape(2 * rows, width),
        [HBM] * 2,
        [pltpu.VMEM((2, rows, width), BF16), pltpu.SemaphoreType.DMA((2,))],
        pltpu.with_memory_space_constraint(tokens, pltpu.HBM),
        pltpu.with_memory_space_constraint(out_cot, pltpu.HBM),
        cost_estimate=long,
    )
    parts = {0: mine}
    for bit in sorted(range(1, col_devices), key=lambda bit: (bit < 4, bit % 2 if bit >= 4 else 0, bit)):
        parts[bit] = swap(parts[bit - 1], "col", 1) if relayed(bit) else swap(mine, "col", bit)
    parts = [parts[bit] for bit in range(col_devices)]

    tile_rows = shape(row_blocks, tok_count, BS)
    tile_cols = shape(col_blocks, tok_count, BS)
    half_cols = shape(col_blocks, half, BS)
    chunk = shape(2 * rows, width)
    acc_rows = pltpu.VMEM((row_blocks + 1, tok_count, BS), F32)
    acc_cols = pltpu.VMEM((col_blocks + 1, tok_count, BS), F32)
    acc_rows_turned = pltpu.VMEM((row_blocks + 1, BS, tok_count), F32)
    acc_cols_turned = pltpu.VMEM((col_blocks + 1, BS, tok_count), F32)
    rows_turned = pltpu.VMEM((row_blocks, BS, tok_count), BF16)
    cols_turned = pltpu.VMEM((col_blocks, BS, tok_count), BF16)
    ANY = pl.BlockSpec(memory_space=pl.ANY)

    def pair_sum(keep, gives, after):
        others = [swap(give, "row", 1) for give in gives]
        total = call(
            add_kernel, "add", half_cols, [VMEM, ANY] + [VMEM] * len(others), [], keep, after, *others
        )
        bit = 2
        while 2 * bit < row_devices:
            total = (total.astype(F32) + swap(total, "row", bit).astype(F32)).astype(BF16)
            bit *= 2
        return total

    last = row_devices // 2
    up_place, up_weight = call(
        fetch_kernel,
        "fetch",
        (shape(slots, dtype=jnp.int32), shape(slots, BS, BS)),
        [HBM, HBM, VMEM],
        [pltpu.SemaphoreType.DMA((2,))],
        up_place,
        up_weight,
        parts[4 if col_devices > 4 else -1],
        out_specs=(SMEM, VMEM),
        cost_estimate=cost,
    )
    features, cotangents, pre_keep, pre_give = call(
        functools.partial(up_kernel, row_blocks, col_blocks),
        "up",
        (tile_rows, tile_rows, half_cols, half_cols),
        [SMEM] + [VMEM] * (1 + len(parts)),
        [acc_cols],
        up_place,
        up_weight,
        *parts,
        cost_estimate=cost,
    )
    pieces = 2
    bounds = [col_blocks * at // pieces for at in range(pieces + 1)]
    act_keep, *act_gives = call(
        functools.partial(act_kernel, col_blocks, row_blocks),
        "act",
        (half_cols,) + tuple(shape(b - a, half, BS) for a, b in zip(bounds, bounds[1:])),
        [SMEM, VMEM, VMEM],
        [rows_turned, acc_cols_turned],
        down_place,
        down_weight,
        cotangents,
        cost_estimate=cost,
    )
    pre_own = pair_sum(pre_keep, [pre_give], pre_keep)
    pre_other = swap(pre_own, "row", last)
    act_own = pair_sum(act_keep, act_gives, act_keep)
    act_other = swap(act_own, "row", last)

    cut = (col_blocks + 1) // 2
    slope, *hidden_own = call(
        gelu_kernel,
        "gelu",
        (shape(col_blocks, half, BS, dtype=F32),)
        + tuple(shape(count, half, BS) for count in (cut, col_blocks - cut)),
        [VMEM, VMEM, ANY],
        [],
        pre_own,
        pre_other,
        act_own,
    )
    hidden, out_terms = call(
        functools.partial(down_kernel, col_blocks, row_blocks),
        "down",
        (tile_cols, tile_rows),
        [SMEM] + [VMEM] * (1 + 2 * len(hidden_own)),
        [acc_rows],
        down_place,
        down_weight,
        *(each for piece in hidden_own for each in (piece, swap(piece, "row", 1))),
        cost_estimate=cost,
    )

    def grads(name, index, turned, right):
        return call(
            grad_kernel,
            name,
            (shape(slots, BS, BS), shape(8, BS, dtype=F32)),
            [SMEM, VMEM, VMEM],
            [
                pltpu.VMEM((slots, BS, BS), BF16),
                pltpu.SemaphoreType.DMA((slots // divisor(slots, 56),)),
            ],
            index,
            turned,
            right,
            out_specs=(HBM, VMEM),
            cost_estimate=cost,
        )

    turned_hidden, turned_features = call(
        turn_kernel,
        "turn",
        (shape(col_blocks, BS, tok_count), shape(row_blocks, BS, tok_count)),
        [VMEM] * 2,
        [],
        hidden,
        features,
    )
    down_grad, down_mark = grads("down_grad", down_place, turned_hidden, cotangents)
    grad_own = call(
        slope_kernel, "slope", half_cols, [VMEM] * 3 + [ANY], [], act_own, act_other, slope, turned_features
    )
    by_way = [bit for bit in range(col_devices) if relayed(bit)]
    direct = [bit for bit in range(col_devices) if not relayed(bit)]
    pre_grad, relay, *chunks = call(
        functools.partial(input_kernel, row_blocks, col_blocks),
        "input",
        (tile_cols, shape(len(by_way), 2 * rows, width)) + (chunk,) * len(direct),
        [SMEM, VMEM, VMEM, VMEM, VMEM],
        [cols_turned, acc_rows_turned],
        up_place,
        up_weight,
        grad_own,
        swap(grad_own, "row", 1),
        out_terms,
        cost_estimate=cost,
    )
    up_grad, up_mark = grads("up_grad", up_place, turned_features, pre_grad)
    later = [bit for bit in direct if bit not in (2,)]
    merged = call(
        functools.partial(merge_kernel, len(later)),
        "merge",
        (chunk,) * len(later),
        [VMEM] * (2 + len(later)),
        [],
        swap(relay, "col", 1),
        down_mark,
        *(chunks[direct.index(bit)] for bit in later),
    )
    chunks = dict(zip(direct, chunks)) | dict(zip(later, merged))
    total = chunks[0].astype(F32)
    for bit in sorted(direct[1:], key=lambda bit: -bit):
        total = total + swap(chunks[bit], "col", bit).astype(F32)
    total = total.astype(BF16)
    return total[:rows], total[rows:], up_grad[None, None], down_grad[None, None]


def solution(mesh):
    placed = (
        P("col", "row"),
        P("row", "col", None, None, None),
        P("row", "col", None),
        P("row", "col", None, None, None),
        P("row", "col", None),
        P("col", "row"),
    )
    return jax.shard_map(
        shards,
        mesh=mesh,
        in_specs=placed,
        out_specs=(
            P("col", "row"),
            P("col", "row"),
            P("row", "col", None, None, None),
            P("row", "col", None, None, None),
        ),
        check_vma=False,
    )
```

```python
import functools

import jax
import jax.numpy as jnp
from jax import lax
from jax.experimental import pallas as pl
from jax.experimental.pallas import tpu as pltpu
from jax.sharding import PartitionSpec as P

FF = 28672
BS = 128
COEF = 0.7978845608
CUBIC = 0.044715
F32 = jnp.float32
BF16 = jnp.bfloat16
VMEM = pl.BlockSpec(memory_space=pltpu.VMEM)
SMEM = pl.BlockSpec(memory_space=pltpu.SMEM)
HBM = pl.BlockSpec(memory_space=pltpu.HBM)


def gelu_value(values):
    inner = COEF * (values + CUBIC * values * values * values)
    return 0.5 * values * (1.0 + jnp.tanh(inner))


def gelu_slope(values):
    tangent = jnp.tanh(COEF * (values + CUBIC * values * values * values))
    return 0.5 * (1.0 + tangent) + 0.5 * values * (1.0 - tangent * tangent) * COEF * (
        1.0 + 3.0 * CUBIC * values * values
    )


def params(megabytes=24):
    return pltpu.CompilerParams(vmem_limit_bytes=megabytes << 20)


def divisor(count, most):
    return max(step for step in range(1, most + 1) if count % step == 0)


class Stream:
    def __init__(self, index_hbm, blocks_hbm, index_ref, blocks_ref, index_sem, sems):
        self.index, self.blocks = index_ref, blocks_ref
        self.index_copy = pltpu.make_async_copy(index_hbm, index_ref, index_sem)
        self.step = blocks_ref.shape[0] // sems.shape[0]
        self.copies = lambda at: pltpu.make_async_copy(
            blocks_hbm.at[pl.ds(at * self.step, self.step)],
            blocks_ref.at[pl.ds(at * self.step, self.step)],
            sems.at[at],
        )
        self.index_copy.start()
        for at in range(sems.shape[0]):
            self.copies(at).start()

    @staticmethod
    def scratch(slots, most):
        return [
            pltpu.SMEM((slots,), jnp.int32),
            pltpu.VMEM((slots, BS, BS), BF16),
            pltpu.SemaphoreType.DMA,
            pltpu.SemaphoreType.DMA((slots // divisor(slots, most),)),
        ]

    def prepare(self):
        self.index_copy.wait()

    def group(self, at):
        self.copies(at).wait()


class Held:
    def __init__(self, index_ref, blocks_ref, most):
        self.index, self.blocks = index_ref, blocks_ref
        self.step = divisor(blocks_ref.shape[0], most)

    def prepare(self):
        pass

    def group(self, at):
        pass


def accumulate(source, leading, trailing, operand_ref, acc):
    acc[...] = jnp.zeros_like(acc)
    source.prepare()

    def group(at, carry):
        source.group(at)
        products = []
        for inner in range(source.step):
            slot = at * source.step + inner
            place = source.index[slot]
            lead = jnp.minimum(place // trailing, leading - 1)
            trail = jnp.where(place < leading * trailing, place % trailing, trailing)
            products.append(
                (trail, jnp.dot(operand_ref[lead], source.blocks[slot], preferred_element_type=F32))
            )
        for trail, product in products:
            acc[trail] += product
        return carry

    lax.fori_loop(0, source.blocks.shape[0] // source.step, group, 0)


def accumulate_turned(source, leading, trailing, operand_ref, turned, acc):
    for at in range(trailing):
        turned[at] = operand_ref[at].T
    acc[...] = jnp.zeros_like(acc)
    source.prepare()

    def group(at, carry):
        source.group(at)
        products = []
        for inner in range(source.step):
            slot = at * source.step + inner
            place = source.index[slot]
            named = place < leading * trailing
            lead = jnp.where(named, place // trailing, leading)
            products.append(
                (lead, jnp.dot(source.blocks[slot], turned[place % trailing], preferred_element_type=F32))
            )
        for lead, product in products:
            acc[lead] += product
        return carry

    lax.fori_loop(0, source.blocks.shape[0] // source.step, group, 0)


def split_halves(core, read, targets, keep_ref, gives):
    half = keep_ref.shape[1]
    places = [(give_ref, at) for give_ref in gives for at in range(give_ref.shape[0])]
    for at, (give_ref, place) in zip(range(targets), places):
        low, high = read(at, 0), read(at, half)
        keep_ref[at] = jnp.where(core == 0, low, high).astype(BF16)
        give_ref[place] = jnp.where(core == 0, high, low).astype(BF16)


def position(axis):
    return lax.axis_index(axis).astype(jnp.int32)


def core():
    return position("row") % 2


def pack_kernel(tokens_ref, cot_ref, mine_ref):
    mine_ref[...] = jnp.concatenate([tokens_ref[...].astype(F32), cot_ref[...].astype(F32)]).astype(BF16)


def fetch_kernel(index_hbm, blocks_hbm, after_ref, index_ref, blocks_ref, sems):
    copies = [
        pltpu.make_async_copy(source, target, sems.at[at])
        for at, (source, target) in enumerate(((index_hbm, index_ref), (blocks_hbm, blocks_ref)))
    ]
    for copy in copies:
        copy.start()
    for copy in copies:
        copy.wait()


def up_kernel(leading, trailing, index_ref, blocks_ref, *refs):
    parts = refs[:-5]
    tokens_ref, cot_ref, keep_ref, give_ref, acc = refs[-5:]
    source = Held(index_ref, blocks_ref, 112)
    rows = parts[0].shape[0] // 2
    for pair in range(len(parts) // 2):
        here = pl.ds(pair * 2 * rows, 2 * rows)
        for at in range(leading):
            lanes = pl.ds(at * BS, BS)
            first = parts[2 * pair][:, lanes].astype(F32)
            second = parts[2 * pair + 1][:, lanes].astype(F32)
            tokens_ref[at, here, :] = jnp.concatenate([first[:rows], second[:rows]]).astype(BF16)
            cot_ref[at, here, :] = jnp.concatenate([first[rows:], second[rows:]]).astype(BF16)
    accumulate(source, leading, trailing, tokens_ref, acc)
    half = keep_ref.shape[1]
    split_halves(core(), lambda at, low: acc[at, low : low + half, :], trailing, keep_ref, [give_ref])


def act_kernel(
    leading, trailing, index_ref, blocks_ref, cot_ref, keep_ref, *refs
):
    gives, (turned, acc) = refs[:-2], refs[-2:]
    accumulate_turned(Held(index_ref, blocks_ref, 112), leading, trailing, cot_ref, turned, acc)
    half = keep_ref.shape[1]

    def read(at, low):
        return acc[at].T[low : low + half]

    split_halves(core(), read, leading, keep_ref, gives)


def join_halves(core, pieces, whole_ref):
    half = whole_ref.shape[1] // 2
    base = 0
    for own_ref, other_ref in pieces:
        for at in range(own_ref.shape[0]):
            own, other = own_ref[at], other_ref[at]
            whole_ref[base + at, :half, :] = jnp.where(core == 0, own, other)
            whole_ref[base + at, half:, :] = jnp.where(core == 0, other, own)
        base += own_ref.shape[0]


def add_kernel(keep_ref, after_ref, *refs):
    others, out_ref = refs[:-1], refs[-1]
    base = 0
    for other_ref in others:
        for at in range(other_ref.shape[0]):
            out_ref[base + at] = (keep_ref[base + at].astype(F32) + other_ref[at].astype(F32)).astype(BF16)
        base += other_ref.shape[0]


def gelu_kernel(own_ref, other_ref, after_ref, slope_ref, *pieces):
    base = 0
    for hidden_ref in pieces:
        for at in range(hidden_ref.shape[0]):
            preact = own_ref[base + at].astype(F32) + other_ref[base + at].astype(F32)
            hidden_ref[at] = gelu_value(preact).astype(BF16)
            slope_ref[base + at] = gelu_slope(preact)
        base += hidden_ref.shape[0]


def slope_kernel(own_ref, other_ref, slope_ref, after_ref, grad_ref):
    for at in range(own_ref.shape[0]):
        act_grad = own_ref[at].astype(F32) + other_ref[at].astype(F32)
        grad_ref[at] = (act_grad * slope_ref[at]).astype(BF16)


def down_kernel(leading, trailing, index_ref, blocks_ref, *refs):
    pieces, (hidden_ref, terms_ref, acc) = refs[:-3], refs[-3:]
    join_halves(core(), list(zip(pieces[::2], pieces[1::2])), hidden_ref)
    accumulate(Held(index_ref, blocks_ref, 112), leading, trailing, hidden_ref, acc)
    for at in range(trailing):
        terms_ref[at] = acc[at].astype(BF16)


def relayed(bit):
    return bit >= 4 and bit % 2 == 1


def input_kernel(
    leading, trailing, index_ref, blocks_ref, own_ref, other_ref, out_terms_ref, grad_ref, relay_ref, *refs
):
    chunks, turned, acc = refs[:-2], refs[-2], refs[-1]
    join_halves(core(), [(own_ref, other_ref)], grad_ref)
    accumulate_turned(Held(index_ref, blocks_ref, 112), leading, trailing, grad_ref, turned, acc)
    devices = relay_ref.shape[0] + len(chunks)
    rows = grad_ref.shape[1] // devices
    for at in range(leading):
        outs, grads = out_terms_ref[at].astype(F32), acc[at].T
        direct, relays = list(chunks), [relay_ref.at[slot] for slot in range(relay_ref.shape[0])]
        for bit in range(devices):
            mine = slice(bit * rows, (bit + 1) * rows)
            target = (relays if relayed(bit) else direct).pop(0)
            target[:, pl.ds(at * BS, BS)] = jnp.concatenate([outs[mine], grads[mine]]).astype(BF16)


def turn_kernel(*refs):
    count = len(refs) // 2
    for source, target in zip(refs[:count], refs[count:]):
        for at in range(source.shape[0]):
            target[at] = source[at].T


def grad_kernel(index_ref, turned_ref, right_ref, out_ref, mark_ref, held, sems):
    leading, trailing = turned_ref.shape[0], right_ref.shape[0]
    slots = index_ref.shape[0]
    step = divisor(slots, 56)

    def out_copy(at):
        here = pl.ds(at * step, step)
        return pltpu.make_async_copy(held.at[here], out_ref.at[here], sems.at[at])

    def group(at, carry):
        for inner in range(step):
            slot = at * step + inner
            place = index_ref[slot]
            lead = jnp.minimum(place // trailing, leading - 1)
            product = jnp.dot(turned_ref[lead], right_ref[place % trailing], preferred_element_type=F32)
            held[slot] = jnp.where(place < leading * trailing, product, 0.0).astype(BF16)
        out_copy(at).start()
        return carry

    lax.fori_loop(0, slots // step, group, 0)
    mark_ref[...] = jnp.zeros_like(mark_ref)
    for at in range(slots // step):
        out_copy(at).wait()


def merge_kernel(count, *refs):
    relay_ref, ins, outs = refs[0], refs[2 : 2 + count], refs[2 + count :]
    slots = relay_ref.shape[0]
    for at in range(count):
        value = ins[at][...]
        if at >= count - slots:
            value = (value.astype(F32) + relay_ref[at - count + slots].astype(F32)).astype(BF16)
        outs[at][...] = value


def shards(tokens, up_blocks, up_index, down_blocks, down_index, out_cot):
    rows, width = tokens.shape
    col_devices, row_devices = lax.axis_size("col"), lax.axis_size("row")
    row_blocks = width // BS
    col_blocks = FF // (BS * col_devices)
    tok_count = rows * col_devices
    half = tok_count // 2
    slots = up_index.shape[2]
    up_weight = pltpu.with_memory_space_constraint(up_blocks[0, 0], pltpu.HBM)
    down_weight = down_blocks[0, 0]
    up_place = pltpu.with_memory_space_constraint(up_index[0, 0], pltpu.HBM)
    down_place = down_index[0, 0]
    cost = pl.CostEstimate(
        flops=2 * slots * BS * BS * tok_count, bytes_accessed=2 * slots * BS * BS, transcendentals=0
    )

    def swap(values, axis, bit):
        count = lax.axis_size(axis)
        return lax.ppermute(values, axis, [(at, at ^ bit) for at in range(count)])

    def call(body, name, outs, ins, scratch, *args, out_specs=None, **more):
        return pl.pallas_call(
            body,
            out_shape=outs,
            in_specs=ins,
            out_specs=out_specs or jax.tree.map(lambda _: VMEM, outs),
            scratch_shapes=scratch,
            compiler_params=params(),
            name=name,
            **more,
        )(*args)

    def shape(*dims, dtype=BF16):
        return jax.ShapeDtypeStruct(dims, dtype)

    long = pl.CostEstimate(flops=0, bytes_accessed=1 << 25, transcendentals=0)
    mine = call(
        pack_kernel,
        "pack",
        shape(2 * rows, width),
        [pl.BlockSpec((rows, width), lambda: (0, 0))] * 2,
        [],
        pltpu.with_memory_space_constraint(tokens, pltpu.HBM),
        pltpu.with_memory_space_constraint(out_cot, pltpu.HBM),
        cost_estimate=long,
    )
    parts = {0: mine}
    for bit in sorted(range(1, col_devices), key=lambda bit: (bit < 4, bit % 2 if bit >= 4 else 0, bit)):
        parts[bit] = swap(parts[bit - 1], "col", 1) if relayed(bit) else swap(mine, "col", bit)
    parts = [parts[bit] for bit in range(col_devices)]

    tile_rows = shape(row_blocks, tok_count, BS)
    tile_cols = shape(col_blocks, tok_count, BS)
    half_cols = shape(col_blocks, half, BS)
    chunk = shape(2 * rows, width)
    acc_rows = pltpu.VMEM((row_blocks + 1, tok_count, BS), F32)
    acc_cols = pltpu.VMEM((col_blocks + 1, tok_count, BS), F32)
    acc_rows_turned = pltpu.VMEM((row_blocks + 1, BS, tok_count), F32)
    acc_cols_turned = pltpu.VMEM((col_blocks + 1, BS, tok_count), F32)
    rows_turned = pltpu.VMEM((row_blocks, BS, tok_count), BF16)
    cols_turned = pltpu.VMEM((col_blocks, BS, tok_count), BF16)
    ANY = pl.BlockSpec(memory_space=pl.ANY)

    def pair_sum(keep, gives, after):
        others = [swap(give, "row", 1) for give in gives]
        total = call(
            add_kernel, "add", half_cols, [VMEM, ANY] + [VMEM] * len(others), [], keep, after, *others
        )
        bit = 2
        while 2 * bit < row_devices:
            total = (total.astype(F32) + swap(total, "row", bit).astype(F32)).astype(BF16)
            bit *= 2
        return total

    last = row_devices // 2
    up_place, up_weight = call(
        fetch_kernel,
        "fetch",
        (shape(slots, dtype=jnp.int32), shape(slots, BS, BS)),
        [HBM, HBM, VMEM],
        [pltpu.SemaphoreType.DMA((2,))],
        up_place,
        up_weight,
        parts[4 if col_devices > 4 else -1],
        out_specs=(SMEM, VMEM),
        cost_estimate=cost,
    )
    features, cotangents, pre_keep, pre_give = call(
        functools.partial(up_kernel, row_blocks, col_blocks),
        "up",
        (tile_rows, tile_rows, half_cols, half_cols),
        [SMEM] + [VMEM] * (1 + len(parts)),
        [acc_cols],
        up_place,
        up_weight,
        *parts,
        cost_estimate=cost,
    )
    pieces = 2
    bounds = [col_blocks * at // pieces for at in range(pieces + 1)]
    act_keep, *act_gives = call(
        functools.partial(act_kernel, col_blocks, row_blocks),
        "act",
        (half_cols,) + tuple(shape(b - a, half, BS) for a, b in zip(bounds, bounds[1:])),
        [SMEM, VMEM, VMEM],
        [rows_turned, acc_cols_turned],
        down_place,
        down_weight,
        cotangents,
        cost_estimate=cost,
    )
    pre_own = pair_sum(pre_keep, [pre_give], pre_keep)
    pre_other = swap(pre_own, "row", last)
    act_own = pair_sum(act_keep, act_gives, act_keep)
    act_other = swap(act_own, "row", last)

    cut = (col_blocks + 1) // 2
    slope, *hidden_own = call(
        gelu_kernel,
        "gelu",
        (shape(col_blocks, half, BS, dtype=F32),)
        + tuple(shape(count, half, BS) for count in (cut, col_blocks - cut)),
        [VMEM, VMEM, ANY],
        [],
        pre_own,
        pre_other,
        act_own,
    )
    hidden, out_terms = call(
        functools.partial(down_kernel, col_blocks, row_blocks),
        "down",
        (tile_cols, tile_rows),
        [SMEM] + [VMEM] * (1 + 2 * len(hidden_own)),
        [acc_rows],
        down_place,
        down_weight,
        *(each for piece in hidden_own for each in (piece, swap(piece, "row", 1))),
        cost_estimate=cost,
    )

    def grads(name, index, turned, right):
        return call(
            grad_kernel,
            name,
            (shape(slots, BS, BS), shape(8, BS, dtype=F32)),
            [SMEM, VMEM, VMEM],
            [
                pltpu.VMEM((slots, BS, BS), BF16),
                pltpu.SemaphoreType.DMA((slots // divisor(slots, 56),)),
            ],
            index,
            turned,
            right,
            out_specs=(HBM, VMEM),
            cost_estimate=cost,
        )

    turned_hidden, turned_features = call(
        turn_kernel,
        "turn",
        (shape(col_blocks, BS, tok_count), shape(row_blocks, BS, tok_count)),
        [VMEM] * 2,
        [],
        hidden,
        features,
    )
    down_grad, down_mark = grads("down_grad", down_place, turned_hidden, cotangents)
    grad_own = call(
        slope_kernel, "slope", half_cols, [VMEM] * 3 + [ANY], [], act_own, act_other, slope, turned_features
    )
    by_way = [bit for bit in range(col_devices) if relayed(bit)]
    direct = [bit for bit in range(col_devices) if not relayed(bit)]
    pre_grad, relay, *chunks = call(
        functools.partial(input_kernel, row_blocks, col_blocks),
        "input",
        (tile_cols, shape(len(by_way), 2 * rows, width)) + (chunk,) * len(direct),
        [SMEM, VMEM, VMEM, VMEM, VMEM],
        [cols_turned, acc_rows_turned],
        up_place,
        up_weight,
        grad_own,
        swap(grad_own, "row", 1),
        out_terms,
        cost_estimate=cost,
    )
    up_grad, up_mark = grads("up_grad", up_place, turned_features, pre_grad)
    later = [bit for bit in direct if bit not in (2,)]
    merged = call(
        functools.partial(merge_kernel, len(later)),
        "merge",
        (chunk,) * len(later),
        [VMEM] * (2 + len(later)),
        [],
        swap(relay, "col", 1),
        down_mark,
        *(chunks[direct.index(bit)] for bit in later),
    )
    chunks = dict(zip(direct, chunks)) | dict(zip(later, merged))
    total = chunks[0].astype(F32)
    for bit in sorted(direct[1:], key=lambda bit: -bit):
        total = total + swap(chunks[bit], "col", bit).astype(F32)
    total = total.astype(BF16)
    return total[:rows], total[rows:], up_grad[None, None], down_grad[None, None]


def solution(mesh):
    placed = (
        P("col", "row"),
        P("row", "col", None, None, None),
        P("row", "col", None),
        P("row", "col", None, None, None),
        P("row", "col", None),
        P("col", "row"),
    )
    return jax.shard_map(
        shards,
        mesh=mesh,
        in_specs=placed,
        out_specs=(
            P("col", "row"),
            P("col", "row"),
            P("row", "col", None, None, None),
            P("row", "col", None, None, None),
        ),
        check_vma=False,
    )
```
